128 devices in a mesh: seq: 64 (over x, z, y_hi, core), batch: 2 (over y_lo).
Axes of the slice: x: 4, y: 4 (y_hi: 2, y_lo: 2; y = y_hi * 2 + y_lo), z: 4, core: 2. Of those that a mesh axis runs over, the one named last changes fastest.
Arguments:
- inputs: bfloat16 [8, 16384, 768], P('batch', 'seq'), may hold values from -6 to 6
- cotangent: bfloat16 [8, 16384, 768], P('batch', 'seq'), may hold values from -16 to 16
- conv_weight: bfloat16 [2, 3, 768, 384], replicated, may hold values from -0.125 to 0.125
- proj_weight: bfloat16 [2, 384, 768], replicated, may hold values from -0.3125 to 0.3125
Outputs:
- outputs: bfloat16 [8, 16384, 768], P('batch', 'seq')
- input_grad: bfloat16 [8, 16384, 768], P('batch', 'seq')
- conv_grad: float32 [2, 3, 768, 384], P(None, None, ('seq', 'batch'))
- proj_grad: float32 [2, 384, 768], P(None, None, ('seq', 'batch'))
The draws below stay inside these ranges and needn't reach their ends.
All inputs are finite; a program needn't handle non-finite values.
Results may differ from the reference program's by a relative error of at most 0.015.
Values may be sent and summed in bfloat16 or wider, within the bound.
No kernel may reach another device: no remote copies, remote signals or barrier semaphores. Data moves between devices by JAX's collectives and lax.ppermute only.
A program may use at most 128 MiB of HBM per device.

```python
import math
import jax
import jax.numpy as jnp
from jax import lax

C = 768
M = 384
NB = 2
BASE_DILATION = 1024
GENOME_BINS = 16384
GENOMES = 8


def with_spikes(drawn, rng, source, target, blocks, factor):
    owner, partner = [(jnp.arange(drawn.shape[axis_at]) // (drawn.shape[axis_at] // blocks)).reshape([-1 if axis == axis_at else 1 for axis in range(drawn.ndim)]) for axis_at in (source, target)]
    chosen = jax.random.permutation(rng, blocks)[partner]
    strong = (owner == chosen) | (owner == (partner + blocks // 2) % blocks)
    return jnp.where(strong, factor * drawn, drawn)


def levels(key, dims, pieces, low, largest):
    loudness = 1.0
    for position, parts in pieces:
        draws = jax.random.uniform(jax.random.fold_in(jax.random.fold_in(key, 6), position), (parts,), jnp.float32, low / len(pieces), largest / len(pieces))
        loudness = loudness * jnp.repeat(jnp.exp(draws), dims[position] // parts).reshape((-1,) + (1,) * (len(dims) - 1 - position))
    return loudness


def noise(stream_key, dims, spread, most, split=(), kind=jnp.bfloat16):
    values = jax.random.normal(stream_key, dims, jnp.float32) * spread
    if len(split) > 0:
        values = levels(stream_key, dims, split, -0.22, 0.18) * values
    return jnp.clip(values, min=-most, max=most).astype(kind)


def bell_draw_with(rng, shape, spread, most, split, heavy, held_as=jnp.bfloat16):
    drawn = spread * jax.random.normal(rng, shape, jnp.float32)
    if split:
        drawn = drawn * levels(rng, shape, split, -0.22, 0.18)
    return jnp.clip(with_spikes(drawn, jax.random.fold_in(rng, 3), *heavy), -most, most).astype(held_as)


def setup_inputs(seed: int = 0) -> dict:
    key_list = jax.random.split(jax.random.key(seed), 5)
    inputs = noise(key_list[0], (GENOMES, GENOME_BINS, C), 1.0, 6.0, ((0, 2), (1, 64)))
    cotangent = bell_draw_with(key_list[1], (GENOMES, GENOME_BINS, C), 1.0, 16.0, ((0, 2), (1, 64)), (1, 2, 64, 4.0))
    conv_weight = noise(key_list[2], (NB, 3, C, M), (3 * C) ** -0.5, 0.125)
    proj_weight = noise(key_list[3], (NB, M, C), M ** -0.5, 0.3125)
    return {"inputs": inputs, "cotangent": cotangent, "conv_weight": conv_weight, "proj_weight": proj_weight}


def gelu_exact(value):
    return 0.5 * value * (1.0 + lax.erf(value / math.sqrt(2.0)))

def gelu_slope(value):
    cdf = 0.5 * (1.0 + lax.erf(value / math.sqrt(2.0)))
    return cdf + value * jnp.exp(-0.5 * value * value) / math.sqrt(2.0 * math.pi)

def flat_rows(array):
    return array.reshape(-1, array.shape[-1])

def inner_rows(left, right):
    return lax.dot_general(flat_rows(left), flat_rows(right), (((0,), (0,)), ((), ())), preferred_element_type=jnp.float32)

def matmul(left, weight):
    result = jnp.dot(flat_rows(left), weight, preferred_element_type=jnp.float32)
    return result.reshape(left.shape[:-1] + (weight.shape[-1],))

def reference(inputs, cotangent, conv_weight, proj_weight):
    state = inputs
    saved_list = []
    for block_number in range(NB):
        block_dilation = BASE_DILATION * 2 ** block_number
        feature_count = gelu_exact(state.astype(jnp.float32)).astype(jnp.bfloat16)
        backward_neighbour = jnp.roll(feature_count, block_dilation, axis=1)
        forward_neighbour = jnp.roll(feature_count, -block_dilation, axis=1)
        pre_act = matmul(backward_neighbour, conv_weight[block_number, 0]) + matmul(feature_count, conv_weight[block_number, 1]) + matmul(forward_neighbour, conv_weight[block_number, 2])
        activ = gelu_exact(pre_act).astype(jnp.bfloat16)
        saved_list.append((state, feature_count, pre_act, activ))
        state = (state.astype(jnp.float32) + matmul(activ, proj_weight[block_number])).astype(jnp.bfloat16)
    outputs = state
    grad = cotangent
    conv_terms = [None] * NB
    proj_terms = [None] * NB
    for block_number in reversed(range(NB)):
        block_dilation = BASE_DILATION * 2 ** block_number
        state_in, feature_count, pre_act, activ = saved_list[block_number]
        back = matmul(grad, proj_weight[block_number].T)
        activation_slope = (back * gelu_slope(pre_act)).astype(jnp.bfloat16)
        forward_neighbour_slope = jnp.roll(activation_slope, -block_dilation, axis=1)
        backward_neighbour_slope = jnp.roll(activation_slope, block_dilation, axis=1)
        conv_terms[block_number] = jnp.stack([inner_rows(feature_count, forward_neighbour_slope), inner_rows(feature_count, activation_slope), inner_rows(feature_count, backward_neighbour_slope)])
        proj_terms[block_number] = inner_rows(activ, grad)
        summed = matmul(forward_neighbour_slope, conv_weight[block_number, 0].T) + matmul(activation_slope, conv_weight[block_number, 1].T) + matmul(backward_neighbour_slope, conv_weight[block_number, 2].T)
        grad = (grad.astype(jnp.float32) + summed * gelu_slope(state_in.astype(jnp.float32))).astype(jnp.bfloat16)
    factor = jnp.float32(1.0 / math.sqrt(GENOMES * GENOME_BINS))
    conv_grad = jnp.stack(conv_terms) * factor
    proj_grad = jnp.stack(proj_terms) * factor
    return (outputs, grad, conv_grad, proj_grad)
```

```python
import math

import jax
import jax.numpy as jnp
from jax import lax
from jax.sharding import Mesh
from jax.sharding import PartitionSpec as P

CHUNKS = 2
RING = ("x", "z")
SEQ = ("x", "z", "yh", "c")
BF = jnp.bfloat16
F32 = jnp.float32


def cdf_of(value):
    return 0.5 * (1.0 + lax.erf(value * (1.0 / math.sqrt(2.0))))


def density_of(value):
    return jnp.exp(-0.5 * value * value) * (1.0 / math.sqrt(2.0 * math.pi))


def dot(left, right):
    return jnp.dot(left, right, preferred_element_type=F32)


def dot_rows(left, right):
    return lax.dot_general(left, right, (((0,), (0,)), ((), ())), preferred_element_type=F32)


def to_rings(block):
    return lax.all_to_all(block, RING, 0, 0, tiled=True)


def shifted(rows, positions, step):
    return jnp.roll(rows, -positions * step, axis=0)


def forward(state, conv, proj, step):
    saved = []
    for b in range(2):
        dist = 2**b
        value = state.astype(F32)
        cdf = cdf_of(value)
        feature = (value * cdf).astype(BF)
        slope_in = cdf + value * density_of(value)
        taps = jnp.concatenate(
            [shifted(feature, -dist, step), feature, shifted(feature, dist, step)], axis=1
        )
        pre = dot(taps, conv[b].reshape(-1, conv.shape[-1]))
        cdf_u = cdf_of(pre)
        activ = (pre * cdf_u).astype(BF)
        slope_u = cdf_u + pre * density_of(pre)
        state = (value + dot(activ, proj[b])).astype(BF)
        saved.append((feature, slope_in, slope_u, activ))
    return state, saved


def backward(b, grad, saved, conv, proj, step):
    feature, slope_in, slope_u, activ = saved
    dist = 2**b
    e = (dot(grad, proj[b].T) * slope_u).astype(BF)
    taps = jnp.concatenate([shifted(e, dist, step), e, shifted(e, -dist, step)], axis=1)
    flat = jnp.concatenate([conv[b, 0], conv[b, 1], conv[b, 2]], axis=1)
    terms = (dot_rows(feature, taps), dot_rows(grad, activ))
    summed = dot(taps, flat.T)
    return (grad.astype(F32) + summed * slope_in).astype(BF), terms


def share_of(partial):
    rows, n = partial.shape
    part = partial.astype(BF).reshape(32, 2, rows // 64, n)
    me = lax.axis_index("c")
    away = lax.dynamic_index_in_dim(part, 1 - me, 1, keepdims=False)
    here = lax.dynamic_index_in_dim(part, me, 1, keepdims=False)
    came = lax.ppermute(away, "c", [(0, 1), (1, 0)])
    both = (here.astype(F32) + came.astype(F32)).astype(BF)
    both = both.reshape(64, -1, 128)
    got = lax.all_to_all(both, ("x", "z", "yh", "yl"), 0, 0, tiled=True)
    return got.astype(F32).sum(0).reshape(rows // 128, n)


def local(inputs, cotangent, conv, proj):
    genomes, bins, chans = inputs.shape
    rows = genomes * bins // 16
    step = rows // CHUNKS

    def cut(block):
        block = block.reshape(16, CHUNKS, step, chans)
        return [block[:, k] for k in range(CHUNKS)]

    def join(parts):
        return jnp.stack(parts, axis=1).reshape(genomes, bins, chans)

    state_in = [to_rings(p).reshape(16 * step, chans) for p in cut(inputs)]
    grads = [to_rings(p).reshape(16 * step, chans) for p in cut(cotangent)]
    outs, saves = [], []
    for part in state_in:
        out, saved = forward(part, conv, proj, step)
        outs.append(to_rings(out.reshape(16, step, chans)))
        saves.append(saved)
    shares = [None, None]
    for b in (1, 0):
        terms = []
        for k in range(CHUNKS):
            grads[k], term = backward(b, grads[k], saves[k][b], conv, proj, step)
            terms.append(term)
        conv_term = sum(t[0] for t in terms)
        proj_term = sum(t[1] for t in terms)
        shares[b] = share_of(jnp.concatenate([conv_term, proj_term], axis=1))
    grad = join([to_rings(g.reshape(16, step, chans)) for g in grads])
    total = genomes * 2 * bins * 64
    factor = jnp.float32(1.0 / math.sqrt(total))
    mids = conv.shape[-1]
    share = jnp.stack(shares) * factor
    conv_out = share[:, :, : 3 * mids].reshape(2, -1, 3, mids).transpose(0, 2, 1, 3)
    proj_out = share[:, :, 3 * mids :].transpose(0, 2, 1)
    return join(outs), grad, conv_out, proj_out


def solution(mesh):
    fine = Mesh(mesh.devices.reshape(4, 4, 2, 2, 2), ("x", "z", "yh", "c", "yl"))
    rows = P("yl", SEQ, None)
    in_specs = (rows, rows, P(), P())
    out_specs = (rows, rows, P(None, None, SEQ + ("yl",), None), P(None, None, SEQ + ("yl",)))
    return jax.shard_map(local, mesh=fine, in_specs=in_specs, out_specs=out_specs, check_vma=False)
```

```python
import functools
import math

import jax
import jax.numpy as jnp
from jax import lax
from jax.experimental import pallas as pl
from jax.experimental.pallas import tpu as pltpu
from jax.sharding import Mesh
from jax.sharding import PartitionSpec as P

RING = ("x", "z")
COLUMN = ("yh", "yl")
SEQ = ("x", "z", "yh", "c")
BF = jnp.bfloat16
F32 = jnp.float32
BLOCK = 256
VMEM_BYTES = 56 * 1024 * 1024


def gelu_parts(value):
    cdf = 0.5 * (1.0 + lax.erf(value * (1.0 / math.sqrt(2.0))))
    density = jnp.exp(-0.5 * value * value) * (1.0 / math.sqrt(2.0 * math.pi))
    return (value * cdf).astype(BF), (cdf + value * density).astype(BF)


def dot(left, right):
    return jnp.dot(left, right, preferred_element_type=F32)


def dot_t(left, right):
    return lax.dot_general(left, right, (((1,), (1,)), ((), ())), preferred_element_type=F32)


def dot_rows(left, right):
    return lax.dot_general(left, right, (((0,), (0,)), ((), ())), preferred_element_type=F32)


def ring_rows(ref, start, count):
    total = ref.shape[0]
    start %= total
    if start + count <= total:
        return ref[start : start + count, :]
    first = total - start
    return jnp.concatenate([ref[start:total, :], ref[: count - first, :]], axis=0)


def forward_kernel(step, x_ref, conv_ref, proj_ref, *refs):
    out_ref, saved, mid_ref = refs[0], (refs[1:5], refs[5:9]), refs[9]
    total = x_ref.shape[0]
    starts = range(0, total, BLOCK)

    def enter(b, start, value):
        rows = slice(start, start + BLOCK)
        feature, slope = gelu_parts(value)
        saved[b][0][rows, :] = feature
        saved[b][1][rows, :] = slope

    for start in starts:
        enter(0, start, x_ref[start : start + BLOCK, :].astype(F32))
    for b in range(2):
        feature_ref, _, activ_ref, slope_ref = saved[b]
        source = x_ref if b == 0 else mid_ref
        shift = step * 2**b
        for start in starts:
            rows = slice(start, start + BLOCK)
            pre = (
                dot(ring_rows(feature_ref, start - shift, BLOCK), conv_ref[b, 0])
                + dot(feature_ref[rows, :], conv_ref[b, 1])
                + dot(ring_rows(feature_ref, start + shift, BLOCK), conv_ref[b, 2])
            )
            activ, slope = gelu_parts(pre)
            activ_ref[rows, :] = activ
            slope_ref[rows, :] = slope
            after = (source[rows, :].astype(F32) + dot(activ, proj_ref[b])).astype(BF)
            if b == 0:
                mid_ref[rows, :] = after
                enter(1, start, after.astype(F32))
            else:
                out_ref[rows, :] = after


def forward(state, conv, proj, step):
    total, chans = state.shape
    mids = conv.shape[-1]
    wide = jax.ShapeDtypeStruct((total, chans), BF)
    thin = jax.ShapeDtypeStruct((total, mids), BF)
    outs = pl.pallas_call(
        functools.partial(forward_kernel, step),
        out_shape=[wide] + [wide, wide, thin, thin] * 2,
        scratch_shapes=[pltpu.VMEM((total, chans), BF)],
        compiler_params=pltpu.CompilerParams(vmem_limit_bytes=VMEM_BYTES),
        name="forward",
    )(state, conv, proj)
    return outs[0], (outs[1:5], outs[5:9])


def backward_kernel(
    b, step, place_ref, grad_ref, feature_ref, slope_in_ref, activ_ref, slope_ref,
    conv_ref, proj_ref, out_ref, part_ref, e_ref, taps_ref, sum_ref, order_ref,
):
    total, mids = e_ref.shape
    chans = grad_ref.shape[1]
    shift = step * 2**b
    starts = range(0, total, BLOCK)
    for start in starts:
        rows = slice(start, start + BLOCK)
        back = dot_t(grad_ref[rows, :], proj_ref[b])
        e_ref[rows, :] = (back * slope_ref[rows, :].astype(F32)).astype(BF)
    for start in starts:
        rows = slice(start, start + BLOCK)
        taps_ref[rows, :mids] = ring_rows(e_ref, start + shift, BLOCK)
        taps_ref[rows, mids : 2 * mids] = e_ref[rows, :]
        taps_ref[rows, 2 * mids :] = ring_rows(e_ref, start - shift, BLOCK)
    for first in range(0, chans, BLOCK):
        some = slice(first, first + BLOCK)
        sum_ref[some, : 3 * mids] = dot_rows(feature_ref[:, some], taps_ref[...])
        sum_ref[some, 3 * mids :] = dot_rows(grad_ref[:, some], activ_ref[...])
    for start in starts:
        rows = slice(start, start + BLOCK)
        summed = sum(
            dot_t(taps_ref[rows, k * mids : (k + 1) * mids], conv_ref[b, k]) for k in range(3)
        )
        grown = grad_ref[rows, :].astype(F32) + summed * slope_in_ref[rows, :].astype(F32)
        out_ref[rows, :] = grown.astype(BF)
    share = chans // 128
    for c in range(2):
        for y in range(4):
            for ring in range(16):
                owner = ((ring * 2 + y // 2) * 2 + c) * 2 + y % 2
                order_ref[ring * share : (ring + 1) * share, :] = sum_ref[
                    owner * share : (owner + 1) * share, :
                ]
            half = (c + place_ref[0]) % 2
            part_ref[half, (y + 4 - place_ref[1]) % 4] = order_ref[...].astype(BF)


def backward(b, grad, saved, conv, proj, step, place):
    total, chans = grad.shape
    mids = conv.shape[-1]
    vmem = pl.BlockSpec(memory_space=pltpu.VMEM)
    rows = 16 * (chans // 128)
    return pl.pallas_call(
        functools.partial(backward_kernel, b, step),
        out_shape=[
            jax.ShapeDtypeStruct((total, chans), BF),
            jax.ShapeDtypeStruct((2, 4, rows, 4 * mids), BF),
        ],
        in_specs=[pl.BlockSpec(memory_space=pltpu.SMEM)] + [vmem] * 7,
        scratch_shapes=[
            pltpu.VMEM((total, mids), BF),
            pltpu.VMEM((total, 3 * mids), BF),
            pltpu.VMEM((chans, 4 * mids), F32),
            pltpu.VMEM((rows, 4 * mids), F32),
        ],
        compiler_params=pltpu.CompilerParams(vmem_limit_bytes=VMEM_BYTES),
        name="backward%d" % b,
    )(place, grad, *saved, conv, proj)


def to_rings(block):
    return lax.all_to_all(block, RING, 0, 0, tiled=True)


def passed(block, axis, distance):
    size = lax.axis_size(axis)
    return lax.ppermute(block, axis, [(i, (i + distance) % size) for i in range(size)])


def total_of(parts):
    out = parts[0].astype(F32)
    for part in parts[1:]:
        out = out + part.astype(F32)
    return out


def share_of(part):
    both = total_of([part[0], passed(part[1], "c", 1)]).astype(BF)
    both = total_of([both[0]] + [passed(both[k], COLUMN, k) for k in (1, 3, 2)]).astype(BF)
    for axis in RING:
        pieces = both.reshape(4, -1, both.shape[-1])
        me = lax.axis_index(axis)

        def piece(k):
            return lax.dynamic_index_in_dim(pieces, (me + k) % 4, 0, keepdims=False)

        both = total_of([piece(0)] + [passed(piece(k), axis, k) for k in (1, 3, 2)])
        if axis == "x":
            both = both.astype(BF)
    return both


def local(inputs, cotangent, conv, proj):
    genomes, bins, chans = inputs.shape
    total = genomes * bins
    step = total // 16
    mids = conv.shape[-1]

    def rings(block):
        return to_rings(block.reshape(16, step, chans)).reshape(total, chans)

    def unring(block):
        return to_rings(block.reshape(16, step, chans)).reshape(genomes, bins, chans)

    place = jnp.stack([lax.axis_index("c"), lax.axis_index(COLUMN)]).astype(jnp.int32)
    state = rings(inputs)
    grad = rings(cotangent)
    out, saved = forward(state, conv, proj, step)
    outputs = unring(out)
    shares = [None, None]
    for b in (1, 0):
        grad, part = backward(b, grad, saved[b], conv, proj, step, place)
        shares[b] = share_of(part)
    input_grad = unring(grad)
    factor = jnp.float32(1.0 / math.sqrt(total * 128))
    share = jnp.stack(shares) * factor
    conv_out = share[:, :, : 3 * mids].reshape(2, -1, 3, mids).transpose(0, 2, 1, 3)
    proj_out = share[:, :, 3 * mids :].transpose(0, 2, 1)
    return outputs, input_grad, conv_out, proj_out


def solution(mesh):
    fine = Mesh(mesh.devices.reshape(4, 4, 2, 2, 2), ("x", "z", "yh", "c", "yl"))
    rows = P("yl", SEQ, None)
    in_specs = (rows, rows, P(), P())
    out_specs = (rows, rows, P(None, None, SEQ + ("yl",), None), P(None, None, SEQ + ("yl",)))
    return jax.shard_map(local, mesh=fine, in_specs=in_specs, out_specs=out_specs, check_vma=False)
```

```python
import functools
import math

import jax
import jax.numpy as jnp
from jax import lax
from jax.experimental import pallas as pl
from jax.experimental.pallas import tpu as pltpu
from jax.sharding import Mesh
from jax.sharding import PartitionSpec as P

RING = ("x", "z")
COLUMN = ("yh", "yl")
SEQ = ("x", "z", "yh", "c")
BF = jnp.bfloat16
F32 = jnp.float32
BLOCK = 256
VMEM_BYTES = 40 * 1024 * 1024


def gelu_parts(value):
    cdf = 0.5 * (1.0 + lax.erf(value * (1.0 / math.sqrt(2.0))))
    density = jnp.exp(-0.5 * value * value) * (1.0 / math.sqrt(2.0 * math.pi))
    return (value * cdf).astype(BF), (cdf + value * density).astype(BF)


def dot(left, right):
    return jnp.dot(left, right, preferred_element_type=F32)


def dot_t(left, right):
    return lax.dot_general(left, right, (((1,), (1,)), ((), ())), preferred_element_type=F32)


def dot_rows(left, right):
    return lax.dot_general(left, right, (((0,), (0,)), ((), ())), preferred_element_type=F32)


def ring_rows(ref, start, count):
    total = ref.shape[0]
    start %= total
    if start + count <= total:
        return ref[start : start + count, :]
    first = total - start
    return jnp.concatenate([ref[start:total, :], ref[: count - first, :]], axis=0)


class Fetched:
    def __init__(self, copy):
        self.copy, self.here = copy, False
        copy.start()

    def get(self):
        if not self.here:
            self.copy.wait()
            self.here = True
        return self.copy.dst_ref


class Sent:
    def __init__(self, source, target, sem):
        self.source = source
        self.copy = pltpu.make_async_copy(source, target, sem)

    def send(self):
        self.copy.start()

    def finish(self):
        self.copy.wait()


def staged_call(body, name, ins, outs, scratch, work, place=None):
    blocks = [x[1] if isinstance(x, tuple) else None for x in ins]
    arrays = [x[0] if isinstance(x, tuple) else x for x in ins]
    shapes = [x.shape if b is None else x.shape[1:] for x, b in zip(arrays, blocks)]
    held = [pltpu.VMEM(shape, BF) for shape in shapes] + [pltpu.VMEM(x.shape, BF) for x in outs]
    n, m, k = len(arrays), len(outs), len(held)
    extra = [] if place is None else [place]

    def kernel(*refs):
        head, refs = refs[: len(extra)], refs[len(extra) :]
        sources, targets, kept = refs[:n], refs[n : n + m], refs[n + m : n + m + k]
        in_sems, out_sems = refs[n + m + k], refs[n + m + k + 1]
        rest = refs[n + m + k + 2 :]
        sources = [ref if b is None else ref.at[b] for ref, b in zip(sources, blocks)]
        fetched = [
            Fetched(pltpu.make_async_copy(sources[i], kept[i], in_sems.at[i])) for i in range(n)
        ]
        sent = [Sent(kept[n + i], targets[i], out_sems.at[i]) for i in range(m)]
        body(fetched, sent, *head, *rest)
        for result in sent:
            result.finish()

    return pl.pallas_call(
        kernel,
        out_shape=[pltpu.HBM(x.shape, x.dtype) for x in outs],
        in_specs=[pl.BlockSpec(memory_space=pltpu.SMEM)] * len(extra)
        + [pl.BlockSpec(memory_space=pltpu.HBM)] * n,
        out_specs=[pl.BlockSpec(memory_space=pltpu.HBM)] * m,
        scratch_shapes=held
        + [pltpu.SemaphoreType.DMA((n,)), pltpu.SemaphoreType.DMA((m,))]
        + list(scratch),
        compiler_params=pltpu.CompilerParams(vmem_limit_bytes=VMEM_BYTES),
        cost_estimate=pl.CostEstimate(flops=1, bytes_accessed=1, transcendentals=0),
        name=name,
    )(*extra, *[pltpu.with_memory_space_constraint(x, pltpu.HBM) for x in arrays])


def forward(state, conv, proj, step):
    total, chans = state.shape
    mids = conv.shape[-1]
    wide = jax.ShapeDtypeStruct((total, chans), BF)
    thin = jax.ShapeDtypeStruct((total, mids), BF)
    starts = range(0, total, BLOCK)

    def body(fetched, sent, mid_ref):
        out, saved = sent[0], (sent[1:5], sent[5:9])

        def enter(b, start, value):
            rows = slice(start, start + BLOCK)
            feature, slope = gelu_parts(value)
            saved[b][0].source[rows, :] = feature
            saved[b][1].source[rows, :] = slope

        x_ref = fetched[0].get()
        for start in starts:
            enter(0, start, x_ref[start : start + BLOCK, :].astype(F32))
        saved[0][0].send()
        saved[0][1].send()
        for b in range(2):
            feature_ref, activ_ref, slope_ref = (saved[b][i].source for i in (0, 2, 3))
            conv_ref, proj_ref = fetched[1 + 2 * b].get(), fetched[2 + 2 * b].get()
            source = x_ref if b == 0 else mid_ref
            shift = step * 2**b
            for start in starts:
                rows = slice(start, start + BLOCK)
                pre = (
                    dot(ring_rows(feature_ref, start - shift, BLOCK), conv_ref[0])
                    + dot(feature_ref[rows, :], conv_ref[1])
                    + dot(ring_rows(feature_ref, start + shift, BLOCK), conv_ref[2])
                )
                activ, slope = gelu_parts(pre)
                activ_ref[rows, :] = activ
                slope_ref[rows, :] = slope
                after = source[rows, :].astype(F32) + dot(activ, proj_ref[...])
                after = after.astype(BF)
                if b == 0:
                    mid_ref[rows, :] = after
                    enter(1, start, after.astype(F32))
                else:
                    out.source[rows, :] = after
            for result in saved[0][2:] + saved[1][:2] if b == 0 else [*saved[1][2:], out]:
                result.send()

    outs = staged_call(
        body, "forward", [state, (conv, 0), (proj, 0), (conv, 1), (proj, 1)],
        [wide] + [wide, wide, thin, thin] * 2, [pltpu.VMEM((total, chans), BF)],
        16 * total * chans * mids,
    )
    return outs[0], (outs[1:5], outs[5:9])


def put_taps(e_ref, taps_ref, shift):
    total, mids = e_ref.shape
    for start in range(0, total, BLOCK):
        rows = slice(start, start + BLOCK)
        taps_ref[rows, :mids] = ring_rows(e_ref, start + shift, BLOCK)
        taps_ref[rows, mids : 2 * mids] = e_ref[rows, :]
        taps_ref[rows, 2 * mids :] = ring_rows(e_ref, start - shift, BLOCK)


def spread(e_ref, conv_ref, start, shift):
    return (
        dot_t(ring_rows(e_ref, start + shift, BLOCK), conv_ref[0])
        + dot_t(e_ref[start : start + BLOCK, :], conv_ref[1])
        + dot_t(ring_rows(e_ref, start - shift, BLOCK), conv_ref[2])
    )


def weight_terms(left_ref, right_ref, sum_ref, at):
    chans, wide = left_ref.shape[1], right_ref.shape[1]
    for first in range(0, chans, BLOCK):
        some = slice(first, first + BLOCK)
        sum_ref[some, at : at + wide] = dot_rows(left_ref[:, some], right_ref[...])


def put_in_order(place_ref, sum_ref, order_ref, mine, away):
    share = sum_ref.shape[0] // 128
    for c in range(2):
        for y in range(4):
            for ring in range(16):
                owner = ((ring * 2 + y // 2) * 2 + c) * 2 + y % 2
                order_ref[ring * share : (ring + 1) * share, :] = sum_ref[
                    owner * share : (owner + 1) * share, :
                ]
            slot = (y + 4 - place_ref[1]) % 4

            @pl.when(place_ref[0] == c)
            def _():
                mine.source[slot] = order_ref[...].astype(BF)

            @pl.when(place_ref[0] != c)
            def _():
                away.source[slot] = order_ref[...].astype(BF)

    away.send()
    mine.send()


def term_scratch(chans, wide):
    return [pltpu.VMEM((chans, wide), F32), pltpu.VMEM((16 * (chans // 128), wide), F32)]


def term_outs(chans, wide):
    return [jax.ShapeDtypeStruct((4, 16 * (chans // 128), wide), BF)] * 2


def later(grad_parts, slope1, feature1, activ1, slope_in1, activ0, conv, proj, step, place):
    total, chans = feature1.shape
    mids = slope1.shape[1]
    starts = range(0, total, BLOCK)

    def body(fetched, sent, place_ref, e_ref, taps_ref, sum_ref, order_ref):
        mid, mine, away = sent
        grad_ref, proj_ref, slope_ref = (f.get() for f in fetched[:3])
        for start in starts:
            rows = slice(start, start + BLOCK)
            pulled = dot_t(grad_ref[rows, :], proj_ref[...])
            e_ref[rows, :] = (pulled * slope_ref[rows, :].astype(F32)).astype(BF)
        put_taps(e_ref, taps_ref, 2 * step)
        conv_ref, slope_in_ref, feature_ref, activ_ref, before_ref = (f.get() for f in fetched[3:])
        for start in starts:
            rows = slice(start, start + BLOCK)
            summed = spread(e_ref, conv_ref, start, 2 * step)
            grown = grad_ref[rows, :].astype(F32) + summed * slope_in_ref[rows, :].astype(F32)
            mid.source[rows, :] = grown.astype(BF)
        mid.send()
        weight_terms(feature_ref, taps_ref, sum_ref, 0)
        weight_terms(grad_ref, activ_ref, sum_ref, 3 * mids)
        weight_terms(mid.source, before_ref, sum_ref, 4 * mids)
        put_in_order(place_ref, sum_ref, order_ref, mine, away)

    return staged_call(
        body, "later",
        [grad_parts, (proj, 1), slope1, (conv, 1), slope_in1, feature1, activ1, activ0],
        [jax.ShapeDtypeStruct((total, chans), BF)] + term_outs(chans, 5 * mids),
        [pltpu.VMEM((total, mids), BF), pltpu.VMEM((total, 3 * mids), BF)]
        + term_scratch(chans, 5 * mids),
        18 * total * chans * mids, place,
    )


def first(mid, slope0, feature0, slope_in0, conv, proj, step, place):
    total, chans = mid.shape
    mids = slope0.shape[1]
    starts = range(0, total, BLOCK)

    def body(fetched, sent, place_ref, e_ref, taps_ref, sum_ref, order_ref):
        out, mine, away = sent
        mid_ref, proj_ref, slope_ref = (f.get() for f in fetched[:3])
        for start in starts:
            rows = slice(start, start + BLOCK)
            pulled = dot_t(mid_ref[rows, :], proj_ref[...])
            e_ref[rows, :] = (pulled * slope_ref[rows, :].astype(F32)).astype(BF)
        put_taps(e_ref, taps_ref, step)
        feature_ref, conv_ref, slope_in_ref = (f.get() for f in fetched[3:])
        weight_terms(feature_ref, taps_ref, sum_ref, 0)
        put_in_order(place_ref, sum_ref, order_ref, mine, away)
        for start in starts:
            rows = slice(start, start + BLOCK)
            summed = spread(e_ref, conv_ref, start, step)
            grown = mid_ref[rows, :].astype(F32) + summed * slope_in_ref[rows, :].astype(F32)
            out.source[rows, :] = grown.astype(BF)
        out.send()

    return staged_call(
        body, "first", [mid, (proj, 0), slope0, feature0, (conv, 0), slope_in0],
        [jax.ShapeDtypeStruct((total, chans), BF)] + term_outs(chans, 3 * mids),
        [pltpu.VMEM((total, mids), BF), pltpu.VMEM((total, 3 * mids), BF)]
        + term_scratch(chans, 3 * mids),
        14 * total * chans * mids, place,
    )


def to_rings(block):
    return lax.all_to_all(block, RING, 0, 0, tiled=True)


def passed(block, axis, distance):
    size = lax.axis_size(axis)
    return lax.ppermute(block, axis, [(i, (i + distance) % size) for i in range(size)])


def total_of(parts):
    out = parts[0].astype(F32)
    for part in parts[1:]:
        out = out + part.astype(F32)
    return out


def column_share(mine, came):
    both = [total_of([mine[k], came[k]]).astype(BF) for k in range(4)]
    return total_of([both[0]] + [passed(both[k], COLUMN, k) for k in (1, 3, 2)]).astype(BF)


def ring_share(both):
    rows, wide = both.shape
    got = lax.all_to_all(both.reshape(16, -1, 128), RING, 0, 0, tiled=True)
    return got.astype(F32).sum(0).reshape(rows // 16, wide)


def local(inputs, cotangent, conv, proj):
    genomes, bins, chans = inputs.shape
    total = genomes * bins
    step = total // 16
    mids = conv.shape[-1]

    def rings(block):
        return to_rings(block.reshape(16, step, chans)).reshape(total, chans)

    def unring(block):
        return to_rings(block.reshape(16, step, chans)).reshape(genomes, bins, chans)

    place = [lax.axis_index("c"), lax.axis_index(COLUMN)]
    place = jnp.stack(place).astype(jnp.int32)
    state = rings(inputs)
    grad = rings(cotangent)
    out, saved = forward(state, conv, proj, step)
    (feature0, slope_in0, activ0, slope0), (feature1, slope_in1, activ1, slope1) = saved
    outputs = unring(out)
    mid, mine1, away1 = later(
        grad, slope1, feature1, activ1, slope_in1, activ0, conv, proj, step, place
    )
    out, mine0, away0 = first(mid, slope0, feature0, slope_in0, conv, proj, step, place)
    input_grad = unring(out)
    came1, came0 = passed(away1, "c", 1), passed(away0, "c", 1)
    came1, came0, outputs = lax.optimization_barrier((came1, came0, outputs))
    both = [column_share(mine0, came0), column_share(mine1, came1)]
    share = ring_share(jnp.concatenate(both, axis=1))
    share = share * jnp.float32(1.0 / math.sqrt(total * 128))
    wide = 3 * mids
    conv_out = jnp.stack([share[:, :wide], share[:, wide : 2 * wide]])
    conv_out = conv_out.reshape(2, -1, 3, mids).transpose(0, 2, 1, 3)
    proj_out = jnp.stack([share[:, 2 * wide + mids :].T, share[:, 2 * wide : 2 * wide + mids].T])
    return outputs, input_grad, conv_out, proj_out


def solution(mesh):
    fine = Mesh(mesh.devices.reshape(4, 4, 2, 2, 2), ("x", "z", "yh", "c", "yl"))
    rows = P("yl", SEQ, None)
    in_specs = (rows, rows, P(), P())
    out_specs = (rows, rows, P(None, None, SEQ + ("yl",), None), P(None, None, SEQ + ("yl",)))
    return jax.shard_map(local, mesh=fine, in_specs=in_specs, out_specs=out_specs, check_vma=False)
```

```python
import functools
import math

import jax
import jax.numpy as jnp
from jax import lax
from jax.experimental import pallas as pl
from jax.experimental.pallas import tpu as pltpu
from jax.sharding import Mesh
from jax.sharding import PartitionSpec as P

RING = ("x", "z")
COLUMN = ("yh", "yl")
SEQ = ("x", "z", "yh", "c")
BF = jnp.bfloat16
F32 = jnp.float32
BLOCK = 256
VMEM_BYTES = 52 * 1024 * 1024


def gelu_parts(value):
    cdf = 0.5 * (1.0 + lax.erf(value * (1.0 / math.sqrt(2.0))))
    density = jnp.exp(-0.5 * value * value) * (1.0 / math.sqrt(2.0 * math.pi))
    return (value * cdf).astype(BF), (cdf + value * density).astype(BF)


def dot(left, right):
    return jnp.dot(left, right, preferred_element_type=F32)


def dot_t(left, right):
    return lax.dot_general(left, right, (((1,), (1,)), ((), ())), preferred_element_type=F32)


def dot_rows(left, right):
    return lax.dot_general(left, right, (((0,), (0,)), ((), ())), preferred_element_type=F32)


def ring_rows(ref, start, count):
    total = ref.shape[0]
    start %= total
    if start + count <= total:
        return ref[start : start + count, :]
    first = total - start
    return jnp.concatenate([ref[start:total, :], ref[: count - first, :]], axis=0)


class Fetched:
    def __init__(self, copies, target):
        self.copies, self.target, self.here = copies, target, False

    def start(self):
        for copy in self.copies:
            copy.start()

    def get(self):
        if not self.here:
            for copy in self.copies:
                copy.wait()
            self.here = True
        return self.target


class Sent:
    def __init__(self, source, copies):
        self.source, self.copies = source, copies

    def send(self):
        for copy in self.copies:
            copy.start()

    def finish(self):
        for copy in self.copies:
            copy.wait()


def get_then(wanted, following):
    refs = [f.get() for f in wanted]
    for f in following:
        f.start()
    return refs


class Flat:
    def __init__(self, array, b):
        self.array, self.b = array, b
        taps, chans, mids = array.shape[1:]
        self.shape = (chans, taps * mids)

    def copies(self, source, target, sems):
        mids = self.array.shape[-1]
        return [
            pltpu.make_async_copy(
                source.at[self.b, k], target.at[:, k * mids : (k + 1) * mids], sems.at[k]
            )
            for k in range(3)
        ]


class Plain:
    def __init__(self, array, b=None, anywhere=False):
        self.array, self.b, self.anywhere = array, b, anywhere
        self.shape = array.shape if b is None else array.shape[1:]

    def copies(self, source, target, sems):
        source = source if self.b is None else source.at[self.b]
        return [pltpu.make_async_copy(source, target, sems.at[0])]


def staged_call(body, name, ins, outs, scratch, urgent, place=None):
    kept_outs = [pltpu.VMEM(shape, BF) for shape, _ in outs]
    held = [pltpu.VMEM(x.shape, BF) for x in ins] + kept_outs
    results = [(i, k) for i, (_, count) in enumerate(outs) for k in range(count or 1)]
    n, m, held_n = len(ins), len(results), len(held)
    extra = [] if place is None else [place]

    def kernel(*refs):
        head, refs = refs[: len(extra)], refs[len(extra) :]
        sources, targets, kept = refs[:n], refs[n : n + m], refs[n + m : n + m + held_n]
        in_sems, out_sems = refs[n + m + held_n], refs[n + m + held_n + 1]
        rest = refs[n + m + held_n + 2 :]
        fetched = [
            Fetched(x.copies(sources[i], kept[i], in_sems.at[i]), kept[i])
            for i, x in enumerate(ins)
        ]
        for f in fetched[:urgent]:
            f.start()
        sent = [Sent(kept[n + i], []) for i in range(len(outs))]
        for j, (i, k) in enumerate(results):
            source = kept[n + i] if outs[i][1] is None else kept[n + i].at[k]
            sent[i].copies.append(pltpu.make_async_copy(source, targets[j], out_sems.at[j]))
        body(fetched, sent, *head, *rest)
        for result in sent:
            result.finish()

    def out_shape(i):
        shape, count = outs[i]
        return pltpu.HBM(shape if count is None else shape[1:], BF)

    return pl.pallas_call(
        kernel,
        out_shape=[out_shape(i) for i, _ in results],
        in_specs=[pl.BlockSpec(memory_space=pltpu.SMEM)] * len(extra)
        + [pl.BlockSpec(memory_space=pl.ANY if anywhere(x) else pltpu.HBM) for x in ins],
        out_specs=[pl.BlockSpec(memory_space=pltpu.HBM)] * m,
        scratch_shapes=held
        + [pltpu.SemaphoreType.DMA((n, 3)), pltpu.SemaphoreType.DMA((m,))]
        + list(scratch),
        compiler_params=pltpu.CompilerParams(vmem_limit_bytes=VMEM_BYTES),
        cost_estimate=pl.CostEstimate(flops=1, bytes_accessed=1, transcendentals=0),
        name=name,
    )(
        *extra,
        *[
            x.array if anywhere(x) else pltpu.with_memory_space_constraint(x.array, pltpu.HBM)
            for x in ins
        ],
    )


def anywhere(operand):
    return getattr(operand, "anywhere", False)


def settled(array):
    return array * lax.optimization_barrier(jnp.ones((), array.dtype))


def forward(state, conv, proj, step):
    total, chans = state.shape
    mids = conv.shape[-1]
    wide, thin = ((total, chans), None), ((total, mids), None)
    starts = range(0, total, BLOCK)

    def body(fetched, sent, mid_ref):
        out, saved = sent[0], (sent[1:5], sent[5:9])

        def enter(b, start, value):
            rows = slice(start, start + BLOCK)
            feature, slope = gelu_parts(value)
            saved[b][0].source[rows, :] = feature
            saved[b][1].source[rows, :] = slope

        (x_ref,) = get_then(fetched[:1], fetched[1:])
        for start in starts:
            enter(0, start, x_ref[start : start + BLOCK, :].astype(F32))
        saved[0][0].send()
        saved[0][1].send()
        for b in range(2):
            feature_ref, activ_ref, slope_ref = (saved[b][i].source for i in (0, 2, 3))
            conv_ref, proj_ref = fetched[1 + 2 * b].get(), fetched[2 + 2 * b].get()
            source = x_ref if b == 0 else mid_ref
            shift = step * 2**b
            for start in starts:
                rows = slice(start, start + BLOCK)
                pre = (
                    dot(ring_rows(feature_ref, start - shift, BLOCK), conv_ref[0])
                    + dot(feature_ref[rows, :], conv_ref[1])
                    + dot(ring_rows(feature_ref, start + shift, BLOCK), conv_ref[2])
                )
                activ, slope = gelu_parts(pre)
                activ_ref[rows, :] = activ
                slope_ref[rows, :] = slope
                after = source[rows, :].astype(F32) + dot(activ, proj_ref[...])
                after = after.astype(BF)
                if b == 0:
                    mid_ref[rows, :] = after
                    enter(1, start, after.astype(F32))
                else:
                    out.source[rows, :] = after
            for result in saved[0][2:] + saved[1][:2] if b == 0 else [*saved[1][2:], out]:
                result.send()

    outs = staged_call(
        body, "forward",
        [Plain(state, anywhere=True)] + [Plain(x, b) for b in range(2) for x in (conv, proj)],
        [wide] + [wide, wide, thin, thin] * 2, [pltpu.VMEM((total, chans), BF)], 1,
    )
    return outs[0], (outs[1:5], outs[5:9])


def put_ring_rows(ref, start, columns, value):
    total, count = ref.shape[0], value.shape[0]
    start %= total
    first = min(count, total - start)
    ref[start : start + first, columns] = value[:first]
    if first < count:
        ref[: count - first, columns] = value[first:]


def pull(from_ref, proj_ref, slope_ref, taps_ref, shift):
    total, mids = slope_ref.shape
    for start in range(0, total, BLOCK):
        rows = slice(start, start + BLOCK)
        pulled = dot_t(from_ref[rows, :], proj_ref[...])
        e = (pulled * slope_ref[rows, :].astype(F32)).astype(BF)
        for k in range(3):
            columns = slice(k * mids, (k + 1) * mids)
            put_ring_rows(taps_ref, start + (k - 1) * shift, columns, e)


def grow(from_ref, taps_ref, flat_ref, slope_ref, out_ref):
    for start in range(0, from_ref.shape[0], BLOCK):
        rows = slice(start, start + BLOCK)
        summed = dot_t(taps_ref[rows, :], flat_ref[...])
        grown = from_ref[rows, :].astype(F32) + summed * slope_ref[rows, :].astype(F32)
        out_ref[rows, :] = grown.astype(BF)


def weight_terms(left_ref, right_ref, sum_ref, at):
    chans, wide = left_ref.shape[1], right_ref.shape[1]
    for first in range(0, chans, BLOCK):
        some = slice(first, first + BLOCK)
        sum_ref[some, at : at + wide] = dot_rows(left_ref[:, some], right_ref[...])


def put_in_order(place_ref, sum_ref, order_ref, part_ref):
    share = sum_ref.shape[0] // 128
    for c in range(2):
        for y in range(4):
            at = order_ref.at[c * 4 + y]
            for ring in range(16):
                owner = ((ring * 2 + y // 2) * 2 + c) * 2 + y % 2
                at[ring * share : (ring + 1) * share, :] = sum_ref[
                    owner * share : (owner + 1) * share, :
                ]
            half, slot = (c + place_ref[0]) % 2, (y + 4 - place_ref[1]) % 4
            part_ref[half, slot] = at[...].astype(BF)


def backward(grad, saved, conv, proj, step, place):
    total, chans = grad.shape
    mids = conv.shape[-1]
    rows, wide = 16 * (chans // 128), 4 * mids
    ins = [Plain(grad, anywhere=True)]
    for b in (1, 0):
        feature, slope_in, activ, slope = saved[b]
        ins += [Plain(proj, b), Plain(slope), Plain(feature), Plain(activ)]
        ins += [Flat(conv, b), Plain(slope_in)]

    def body(fetched, sent, place_ref, grown_ref, taps_ref, sum_ref, order_ref):
        (grad_ref,), queue = get_then(fetched[:1], []), fetched[1:] + [None] * 6
        for b in (1, 0):
            mine, queue = queue[:6], queue[6:]
            ahead = [f for f in queue[:6] if f is not None]
            out_ref = grown_ref if b == 1 else sent[0].source
            proj_ref, slope_ref = get_then(mine[:2], mine[2:] if b == 1 else [])
            pull(grad_ref, proj_ref, slope_ref, taps_ref, step * 2**b)
            feature_ref, activ_ref = get_then(mine[2:4], [])
            weight_terms(feature_ref, taps_ref, sum_ref, 0)
            weight_terms(grad_ref, activ_ref, sum_ref, 3 * mids)
            flat_ref, slope_in_ref = get_then(mine[4:], ahead)
            grow(grad_ref, taps_ref, flat_ref, slope_in_ref, out_ref)
            if b == 0:
                sent[0].send()
            put_in_order(place_ref, sum_ref, order_ref, sent[2 - b].source)
            sent[2 - b].send()
            grad_ref = out_ref

    part = ((2, 4, rows, wide), 2)
    return staged_call(
        body, "backward", ins, [((total, chans), None), part, part],
        [
            pltpu.VMEM((total, chans), BF),
            pltpu.VMEM((total, 3 * mids), BF),
            pltpu.VMEM((chans, wide), F32),
            pltpu.VMEM((8, rows, wide), F32),
        ],
        3, place,
    )


def to_rings(block):
    return lax.all_to_all(block, RING, 0, 0, tiled=True)


def passed(block, axis, distance):
    size = lax.axis_size(axis)
    return lax.ppermute(block, axis, [(i, (i + distance) % size) for i in range(size)])


def total_of(parts):
    out = parts[0].astype(F32)
    for part in parts[1:]:
        out = out + part.astype(F32)
    return out


def column_share(mine, came):
    both = [total_of([mine[k], came[k]]).astype(BF) for k in range(4)]
    return total_of([both[0]] + [passed(both[k], COLUMN, k) for k in (1, 3, 2)]).astype(BF)


def ring_step(both, axis):
    pieces = both.reshape(4, -1, both.shape[-1])
    me = lax.axis_index(axis)

    def piece(k):
        return lax.dynamic_index_in_dim(pieces, (me + k) % 4, 0, keepdims=False)

    return total_of([piece(0)] + [passed(piece(k), axis, k) for k in (2, 1, 3)])


def local(inputs, cotangent, conv, proj):
    genomes, bins, chans = inputs.shape
    total = genomes * bins
    step = total // 16
    mids = conv.shape[-1]

    def rings(block):
        return to_rings(block.reshape(16, step, chans)).reshape(total, chans)

    def unring(block):
        return to_rings(block.reshape(16, step, chans)).reshape(genomes, bins, chans)

    place = [lax.axis_index("c"), lax.axis_index(COLUMN)]
    place = jnp.stack(place).astype(jnp.int32)
    state = rings(inputs)
    grad = rings(cotangent)
    out, saved = forward(state, conv, proj, step)
    outputs = unring(out)
    grad, mine1, away1, mine0, away0 = backward(grad, saved, conv, proj, step, place)
    input_grad = unring(grad)
    came0, came1 = passed(away0, "c", 1), passed(away1, "c", 1)
    came0, came1, outputs = lax.optimization_barrier((came0, came1, outputs))
    early, late = column_share(mine0, came0), column_share(mine1, came1)
    share = ring_step(jnp.concatenate([early, late], axis=1), "x").astype(BF)
    outputs, input_grad = settled(outputs), settled(input_grad)
    share, outputs, input_grad = lax.optimization_barrier((share, outputs, input_grad))
    share = ring_step(share, "z")
    share = share * jnp.float32(1.0 / math.sqrt(total * 128))
    wide = 3 * mids
    share = share.reshape(-1, 2, 4, mids)
    conv_out = share[:, :, :3].transpose(1, 2, 0, 3)
    proj_out = share[:, :, 3].transpose(1, 2, 0)
    return outputs, input_grad, conv_out, proj_out


def solution(mesh):
    fine = Mesh(mesh.devices.reshape(4, 4, 2, 2, 2), ("x", "z", "yh", "c", "yl"))
    rows = P("yl", SEQ, None)
    in_specs = (rows, rows, P(), P())
    out_specs = (rows, rows, P(None, None, SEQ + ("yl",), None), P(None, None, SEQ + ("yl",)))
    return jax.shard_map(local, mesh=fine, in_specs=in_specs, out_specs=out_specs, check_vma=False)
```

```python
import functools
import math

import jax
import jax.numpy as jnp
import numpy as np
from jax import lax
from jax.experimental import pallas as pl
from jax.experimental.pallas import tpu as pltpu
from jax.sharding import Mesh
from jax.sharding import PartitionSpec as P

RING = ("x", "z")
COLUMN = ("yh", "yl")
SEQ = ("x", "z", "yh", "c")
BF = jnp.bfloat16
F32 = jnp.float32
BLOCK = 256
VMEM_BYTES = 52 * 1024 * 1024


def gelu_parts(value):
    cdf = 0.5 * (1.0 + lax.erf(value * (1.0 / math.sqrt(2.0))))
    density = jnp.exp(-0.5 * value * value) * (1.0 / math.sqrt(2.0 * math.pi))
    return (value * cdf).astype(BF), (cdf + value * density).astype(BF)


def dot(left, right):
    return jnp.dot(left, right, preferred_element_type=F32)


def dot_t(left, right):
    return lax.dot_general(left, right, (((1,), (1,)), ((), ())), preferred_element_type=F32)


def dot_rows(left, right):
    return lax.dot_general(left, right, (((0,), (0,)), ((), ())), preferred_element_type=F32)


def ring_rows(ref, start, count):
    total = ref.shape[0]
    start %= total
    if start + count <= total:
        return ref[start : start + count, :]
    first = total - start
    return jnp.concatenate([ref[start:total, :], ref[: count - first, :]], axis=0)


class Fetched:
    def __init__(self, copies, target):
        self.copies, self.target, self.here = copies, target, False

    def start(self):
        for copy in self.copies:
            copy.start()

    def get(self):
        if not self.here:
            for copy in self.copies:
                copy.wait()
            self.here = True
        return self.target


class Sent:
    def __init__(self, source, copies):
        self.source, self.copies = source, copies

    def send(self):
        for copy in self.copies:
            copy.start()

    def finish(self):
        for copy in self.copies:
            copy.wait()


def get_then(wanted, following):
    refs = [f.get() for f in wanted]
    for f in following:
        f.start()
    return refs


class Flat:
    def __init__(self, array, b):
        self.array, self.b = array, b
        taps, chans, mids = array.shape[1:]
        self.shape = (chans, taps * mids)

    def copies(self, source, target, sems):
        mids = self.array.shape[-1]
        return [
            pltpu.make_async_copy(
                source.at[self.b, k], target.at[:, k * mids : (k + 1) * mids], sems.at[k]
            )
            for k in range(3)
        ]


class Plain:
    def __init__(self, array, b=None, anywhere=False):
        self.array, self.b, self.anywhere = array, b, anywhere
        self.shape = array.shape if b is None else array.shape[1:]

    def copies(self, source, target, sems):
        source = source if self.b is None else source.at[self.b]
        return [pltpu.make_async_copy(source, target, sems.at[0])]


def staged_call(body, name, ins, outs, scratch, urgent, place=None):
    kept_outs = [pltpu.VMEM(shape, BF) for shape, _ in outs]
    held = [pltpu.VMEM(x.shape, BF) for x in ins] + kept_outs
    results = [(i, k) for i, (_, count) in enumerate(outs) for k in range(count or 1)]
    n, m, held_n = len(ins), len(results), len(held)
    extra = [] if place is None else [place]

    def kernel(*refs):
        head, refs = refs[: len(extra)], refs[len(extra) :]
        sources, targets, kept = refs[:n], refs[n : n + m], refs[n + m : n + m + held_n]
        in_sems, out_sems = refs[n + m + held_n], refs[n + m + held_n + 1]
        rest = refs[n + m + held_n + 2 :]
        fetched = [
            Fetched(x.copies(sources[i], kept[i], in_sems.at[i]), kept[i])
            for i, x in enumerate(ins)
        ]
        for f in fetched[:urgent]:
            f.start()
        sent = [Sent(kept[n + i], []) for i in range(len(outs))]
        for j, (i, k) in enumerate(results):
            source = kept[n + i] if outs[i][1] is None else kept[n + i].at[k]
            sent[i].copies.append(pltpu.make_async_copy(source, targets[j], out_sems.at[j]))
        body(fetched, sent, *head, *rest)
        for result in sent:
            result.finish()

    def out_shape(i):
        shape, count = outs[i]
        return pltpu.HBM(shape if count is None else shape[1:], BF)

    return pl.pallas_call(
        kernel,
        out_shape=[out_shape(i) for i, _ in results],
        in_specs=[pl.BlockSpec(memory_space=pltpu.SMEM)] * len(extra)
        + [pl.BlockSpec(memory_space=pl.ANY if anywhere(x) else pltpu.HBM) for x in ins],
        out_specs=[pl.BlockSpec(memory_space=pltpu.HBM)] * m,
        scratch_shapes=held
        + [pltpu.SemaphoreType.DMA((n, 3)), pltpu.SemaphoreType.DMA((m,))]
        + list(scratch),
        compiler_params=pltpu.CompilerParams(vmem_limit_bytes=VMEM_BYTES),
        cost_estimate=pl.CostEstimate(flops=1, bytes_accessed=1, transcendentals=0),
        name=name,
    )(
        *extra,
        *[
            x.array if anywhere(x) else pltpu.with_memory_space_constraint(x.array, pltpu.HBM)
            for x in ins
        ],
    )


def anywhere(operand):
    return getattr(operand, "anywhere", False)


def settled(array):
    return array * lax.optimization_barrier(jnp.ones((), array.dtype))


def owner_of(c, y, q):
    ring = q if c == 0 else q % 4 * 4 + q // 4
    return ((ring * 2 + y // 2) * 2 + c) * 2 + y % 2


def order_of(chans):
    share = chans // 128
    owners = [owner_of(c, y, q) for c in range(2) for y in range(4) for q in range(16)]
    source = np.repeat(np.array(owners) * share, share) + np.tile(np.arange(share), 128)
    return jnp.asarray(np.arange(chans)[:, None] == source[None, :], BF)


def forward(state, conv, proj, step):
    total, chans = state.shape
    mids = conv.shape[-1]
    wide, thin = ((total, chans), None), ((total, mids), None)
    starts = range(0, total, BLOCK)

    def body(fetched, sent, mid_ref, *feature_refs):
        out, saved = sent[0], (sent[1:5], sent[5:9])

        def enter(b, start, value):
            rows = slice(start, start + BLOCK)
            feature, slope = gelu_parts(value)
            feature_refs[b][rows, :] = feature
            saved[b][0].source[rows, :] = dot(feature, order_ref[...]).astype(BF)
            saved[b][1].source[rows, :] = slope

        x_ref, order_ref = get_then(fetched[:2], fetched[2:])
        for start in starts:
            enter(0, start, x_ref[start : start + BLOCK, :].astype(F32))
        saved[0][0].send()
        saved[0][1].send()
        for b in range(2):
            feature_ref = feature_refs[b]
            activ_ref, slope_ref = saved[b][2].source, saved[b][3].source
            conv_ref, proj_ref = (f.get() for f in fetched[2 + 2 * b : 4 + 2 * b])
            source = x_ref if b == 0 else mid_ref
            shift = step * 2**b
            for start in starts:
                rows = slice(start, start + BLOCK)
                pre = (
                    dot(ring_rows(feature_ref, start - shift, BLOCK), conv_ref[0])
                    + dot(feature_ref[rows, :], conv_ref[1])
                    + dot(ring_rows(feature_ref, start + shift, BLOCK), conv_ref[2])
                )
                activ, slope = gelu_parts(pre)
                activ_ref[rows, :] = activ
                slope_ref[rows, :] = slope
                after = source[rows, :].astype(F32) + dot(activ, proj_ref[...])
                after = after.astype(BF)
                if b == 0:
                    mid_ref[rows, :] = after
                    enter(1, start, after.astype(F32))
                else:
                    out.source[rows, :] = after
            for result in saved[0][2:] + saved[1][:2] if b == 0 else [*saved[1][2:], out]:
                result.send()

    outs = staged_call(
        body, "forward",
        [Plain(state, anywhere=True), Plain(order_of(chans))]
        + [Plain(x, b) for b in range(2) for x in (conv, proj)],
        [wide] + [wide, wide, thin, thin] * 2, [pltpu.VMEM((total, chans), BF)] * 3, 2,
    )
    return outs[0], (outs[1:5], outs[5:9])


def put_ring_rows(ref, start, columns, value):
    total, count = ref.shape[0], value.shape[0]
    start %= total
    first = min(count, total - start)
    ref[start : start + first, columns] = value[:first]
    if first < count:
        ref[: count - first, columns] = value[first:]


def pull(from_ref, proj_ref, slope_ref, taps_ref, shift):
    total, mids = slope_ref.shape
    for start in range(0, total, BLOCK):
        rows = slice(start, start + BLOCK)
        pulled = dot_t(from_ref[rows, :], proj_ref[...])
        e = (pulled * slope_ref[rows, :].astype(F32)).astype(BF)
        for k in range(3):
            columns = slice(k * mids, (k + 1) * mids)
            put_ring_rows(taps_ref, start + (k - 1) * shift, columns, e)


def grow(from_ref, taps_ref, flat_ref, slope_ref, out_ref):
    for start in range(0, from_ref.shape[0], BLOCK):
        rows = slice(start, start + BLOCK)
        summed = dot_t(taps_ref[rows, :], flat_ref[...])
        grown = from_ref[rows, :].astype(F32) + summed * slope_ref[rows, :].astype(F32)
        out_ref[rows, :] = grown.astype(BF)


def slot_of(place_ref, c, y):
    half, slot = (c + place_ref[0]) % 2, (y + 4 - place_ref[1]) % 4
    return half * 2 + slot % 2, slot // 2


def conv_terms(place_ref, feature_ref, taps_ref, part_ref, at):
    chans, wide = feature_ref.shape[1], taps_ref.shape[1]
    rows = chans // 8
    for c in range(2):
        half = slice(4 * c * rows, 4 * (c + 1) * rows)
        terms = dot_rows(feature_ref[:, half], taps_ref[...]).astype(BF)
        for y in range(4):
            pair, slot = slot_of(place_ref, c, y)
            part_ref[pair, slot, :, at : at + wide] = terms[y * rows : (y + 1) * rows]


def proj_terms(place_ref, grad_ref, activ_ref, part_ref, at, sum_ref, order_ref):
    chans, wide = grad_ref.shape[1], activ_ref.shape[1]
    share = chans // 128
    sum_ref[...] = dot_rows(grad_ref[...], activ_ref[...])
    for c in range(2):
        for y in range(4):
            ordered = order_ref.at[c * 4 + y]
            for q in range(16):
                owner = owner_of(c, y, q)
                ordered[q * share : (q + 1) * share, :] = sum_ref[
                    owner * share : (owner + 1) * share, :
                ]
            pair, slot = slot_of(place_ref, c, y)
            part_ref[pair, slot, :, at : at + wide] = ordered[...].astype(BF)


def backward(grad, saved, conv, proj, step, place):
    total, chans = grad.shape
    mids = conv.shape[-1]
    rows = 16 * (chans // 128)
    ins = [Plain(grad, anywhere=True)]
    for b in (1, 0):
        feature, slope_in, activ, slope = saved[b]
        ins += [Plain(proj, b), Plain(slope), Plain(feature), Plain(activ)]
        ins += [Flat(conv, b), Plain(slope_in)]

    def body(fetched, sent, place_ref, grown_ref, taps_ref, sum_ref, order_ref):
        (grad_ref,), queue = get_then(fetched[:1], []), fetched[1:]
        out, part = sent
        for b in (1, 0):
            mine, queue = queue[:6], queue[6:]
            out_ref = grown_ref if b == 1 else out.source
            at = 4 * mids * b
            proj_ref, slope_ref = get_then(mine[:2], mine[2:] if b == 1 else [])
            pull(grad_ref, proj_ref, slope_ref, taps_ref, step * 2**b)
            feature_ref, activ_ref = get_then(mine[2:4], [])
            conv_terms(place_ref, feature_ref, taps_ref, part.source, at)
            proj_terms(
                place_ref, grad_ref, activ_ref, part.source, at + 3 * mids, sum_ref, order_ref
            )
            if b == 0:
                part.send()
            flat_ref, slope_in_ref = get_then(mine[4:], queue)
            grow(grad_ref, taps_ref, flat_ref, slope_in_ref, out_ref)
            grad_ref = out_ref
        out.send()

    return staged_call(
        body, "backward", ins, [((total, chans), None), ((4, 2, rows, 8 * mids), 4)],
        [
            pltpu.VMEM((total, chans), BF),
            pltpu.VMEM((total, 3 * mids), BF),
            pltpu.VMEM((chans, mids), F32),
            pltpu.VMEM((8, rows, mids), F32),
        ],
        3, place,
    )


def to_rings(block):
    return lax.all_to_all(block, RING, 0, 0, tiled=True)


def passed(block, axis, distance):
    size = lax.axis_size(axis)
    return lax.ppermute(block, axis, [(i, (i + distance) % size) for i in range(size)])


def total_of(parts):
    out = parts[0].astype(F32)
    for part in parts[1:]:
        out = out + part.astype(F32)
    return out


def core_sum(mine, came):
    return [total_of([mine[k % 2][k // 2], came[k % 2][k // 2]]).astype(BF) for k in range(4)]


def column_sum(both):
    return total_of([both[0]] + [passed(both[k], COLUMN, k) for k in (2, 1, 3)]).astype(BF)


def ring_step(rows, second):
    pieces = rows.reshape(4, -1, rows.shape[-1])
    x, z, c = (lax.axis_index(axis) for axis in ("x", "z", "c"))
    me = jnp.where(c == second, x, z)

    def piece(k):
        return lax.dynamic_index_in_dim(pieces, (me + k) % 4, 0, keepdims=False)

    def sent(k):
        route = []
        for i in range(32):
            x, z, c = i // 8, i // 2 % 4, i % 2
            x, z = ((x + k) % 4, z) if c == second else (x, (z + k) % 4)
            route.append((i, (x * 4 + z) * 2 + c))
        return lax.ppermute(piece(k), ("x", "z", "c"), route)

    return total_of([piece(0)] + [sent(k) for k in (2, 1, 3)])


def local(inputs, cotangent, conv, proj):
    genomes, bins, chans = inputs.shape
    total = genomes * bins
    step = total // 16
    mids = conv.shape[-1]

    def rings(block):
        return to_rings(block.reshape(16, step, chans)).reshape(total, chans)

    def unring(block):
        return to_rings(block.reshape(16, step, chans)).reshape(genomes, bins, chans)

    place = [lax.axis_index("c"), lax.axis_index(COLUMN)]
    place = jnp.stack(place).astype(jnp.int32)
    state = rings(inputs)
    grad = rings(cotangent)
    out, saved = forward(state, conv, proj, step)
    outputs = unring(out)
    grad, *parts = backward(grad, saved, conv, proj, step, place)
    input_grad = unring(grad)
    came = [passed(part, "c", 1) for part in parts[:1:-1]][::-1]
    *came, outputs = lax.optimization_barrier((*came, outputs))
    share = ring_step(column_sum(core_sum(parts[:2], came)), 0).astype(BF)
    outputs, input_grad = settled(outputs), settled(input_grad)
    share, outputs, input_grad = lax.optimization_barrier((share, outputs, input_grad))
    share = ring_step(share, 1)
    share = share * jnp.float32(1.0 / math.sqrt(total * 128))
    wide = 3 * mids
    share = share.reshape(-1, 2, 4, mids)
    conv_out = share[:, :, :3].transpose(1, 2, 0, 3)
    proj_out = share[:, :, 3].transpose(1, 2, 0)
    return outputs, input_grad, conv_out, proj_out


def solution(mesh):
    fine = Mesh(mesh.devices.reshape(4, 4, 2, 2, 2), ("x", "z", "yh", "c", "yl"))
    rows = P("yl", SEQ, None)
    in_specs = (rows, rows, P(), P())
    out_specs = (rows, rows, P(None, None, SEQ + ("yl",), None), P(None, None, SEQ + ("yl",)))
    return jax.shard_map(local, mesh=fine, in_specs=in_specs, out_specs=out_specs, check_vma=False)
```

```python
import functools
import math

import jax
import jax.numpy as jnp
import numpy as np
from jax import lax
from jax.experimental import pallas as pl
from jax.experimental.pallas import tpu as pltpu
from jax.sharding import Mesh
from jax.sharding import PartitionSpec as P

RING = ("x", "z")
COLUMN = ("yh", "yl")
SEQ = ("x", "z", "yh", "c")
BF = jnp.bfloat16
F32 = jnp.float32
BLOCK = 256
VMEM_BYTES = 52 * 1024 * 1024


def gelu_parts(value):
    cdf = 0.5 * (1.0 + lax.erf(value * (1.0 / math.sqrt(2.0))))
    density = jnp.exp(-0.5 * value * value) * (1.0 / math.sqrt(2.0 * math.pi))
    return (value * cdf).astype(BF), (cdf + value * density).astype(BF)


def dot(left, right):
    return jnp.dot(left, right, preferred_element_type=F32)


def dot_t(left, right):
    return lax.dot_general(left, right, (((1,), (1,)), ((), ())), preferred_element_type=F32)


def dot_rows(left, right):
    return lax.dot_general(left, right, (((0,), (0,)), ((), ())), preferred_element_type=F32)


def ring_rows(ref, start, count):
    total = ref.shape[0]
    start %= total
    if start + count <= total:
        return ref[start : start + count, :]
    first = total - start
    return jnp.concatenate([ref[start:total, :], ref[: count - first, :]], axis=0)


class Fetched:
    def __init__(self, copies, target):
        self.copies, self.target, self.here = copies, target, False

    def start(self):
        for copy in self.copies:
            copy.start()

    def get(self):
        if not self.here:
            for copy in self.copies:
                copy.wait()
            self.here = True
        return self.target


class Sent:
    def __init__(self, source, copies):
        self.source, self.copies = source, copies

    def send(self):
        for copy in self.copies:
            copy.start()

    def finish(self):
        for copy in self.copies:
            copy.wait()


def get_then(wanted, following):
    refs = [f.get() for f in wanted]
    for f in following:
        f.start()
    return refs


class Flat:
    def __init__(self, array, b):
        self.array, self.b = array, b
        taps, chans, mids = array.shape[1:]
        self.shape = (chans, taps * mids)

    def copies(self, source, target, sems):
        mids = self.array.shape[-1]
        return [
            pltpu.make_async_copy(
                source.at[self.b, k], target.at[:, k * mids : (k + 1) * mids], sems.at[k]
            )
            for k in range(3)
        ]


class Plain:
    def __init__(self, array, b=None, anywhere=False):
        self.array, self.b, self.anywhere = array, b, anywhere
        self.shape = array.shape if b is None else array.shape[1:]

    def copies(self, source, target, sems):
        source = source if self.b is None else source.at[self.b]
        return [pltpu.make_async_copy(source, target, sems.at[0])]


def staged_call(body, name, ins, outs, scratch, urgent, place=None):
    kept_outs = [pltpu.VMEM(shape, BF) for shape, _ in outs]
    held = [pltpu.VMEM(x.shape, BF) for x in ins] + kept_outs
    results = [(i, k) for i, (_, count) in enumerate(outs) for k in range(count or 1)]
    n, m, held_n = len(ins), len(results), len(held)
    extra = [] if place is None else [place]

    def kernel(*refs):
        head, refs = refs[: len(extra)], refs[len(extra) :]
        sources, targets, kept = refs[:n], refs[n : n + m], refs[n + m : n + m + held_n]
        in_sems, out_sems = refs[n + m + held_n], refs[n + m + held_n + 1]
        rest = refs[n + m + held_n + 2 :]
        fetched = [
            Fetched(x.copies(sources[i], kept[i], in_sems.at[i]), kept[i])
            for i, x in enumerate(ins)
        ]
        for f in fetched[:urgent]:
            f.start()
        sent = [Sent(kept[n + i], []) for i in range(len(outs))]
        for j, (i, k) in enumerate(results):
            source = kept[n + i] if outs[i][1] is None else kept[n + i].at[k]
            sent[i].copies.append(pltpu.make_async_copy(source, targets[j], out_sems.at[j]))
        body(fetched, sent, *head, *rest)
        for result in sent:
            result.finish()

    def out_shape(i):
        shape, count = outs[i]
        return pltpu.HBM(shape if count is None else shape[1:], BF)

    return pl.pallas_call(
        kernel,
        out_shape=[out_shape(i) for i, _ in results],
        in_specs=[pl.BlockSpec(memory_space=pltpu.SMEM)] * len(extra)
        + [pl.BlockSpec(memory_space=pl.ANY if anywhere(x) else pltpu.HBM) for x in ins],
        out_specs=[pl.BlockSpec(memory_space=pltpu.HBM)] * m,
        scratch_shapes=held
        + [pltpu.SemaphoreType.DMA((n, 3)), pltpu.SemaphoreType.DMA((m,))]
        + list(scratch),
        compiler_params=pltpu.CompilerParams(vmem_limit_bytes=VMEM_BYTES),
        cost_estimate=pl.CostEstimate(flops=1, bytes_accessed=1, transcendentals=0),
        name=name,
    )(
        *extra,
        *[
            x.array if anywhere(x) else pltpu.with_memory_space_constraint(x.array, pltpu.HBM)
            for x in ins
        ],
    )


def anywhere(operand):
    return getattr(operand, "anywhere", False)


def settled(array):
    return array * lax.optimization_barrier(jnp.ones((), array.dtype))


def owner_of(c, y, q):
    ring = q if c == 0 else q % 4 * 4 + q // 4
    return ((ring * 2 + y // 2) * 2 + c) * 2 + y % 2


def order_of(chans):
    share = chans // 128
    owners = [owner_of(c, y, q) for c in range(2) for y in range(4) for q in range(16)]
    source = np.repeat(np.array(owners) * share, share) + np.tile(np.arange(share), 128)
    return jnp.asarray(np.arange(chans)[:, None] == source[None, :], BF)


def forward(state, conv, proj, step):
    total, chans = state.shape
    mids = conv.shape[-1]
    wide, thin = ((total, chans), None), ((total, mids), None)
    starts = range(0, total, BLOCK)

    def body(fetched, sent, mid_ref, *feature_refs):
        out, saved = sent[0], (sent[1:5], sent[5:9])

        def enter(b, start, value):
            rows = slice(start, start + BLOCK)
            feature, slope = gelu_parts(value)
            feature_refs[b][rows, :] = feature
            saved[b][0].source[rows, :] = dot(feature, order_ref[...]).astype(BF)
            saved[b][1].source[rows, :] = slope

        x_ref, order_ref = get_then(fetched[:2], fetched[2:])
        for start in starts:
            enter(0, start, x_ref[start : start + BLOCK, :].astype(F32))
        saved[0][0].send()
        saved[0][1].send()
        for b in range(2):
            feature_ref = feature_refs[b]
            activ_ref, slope_ref = saved[b][2].source, saved[b][3].source
            conv_ref, proj_ref = (f.get() for f in fetched[2 + 2 * b : 4 + 2 * b])
            source = x_ref if b == 0 else mid_ref
            shift = step * 2**b
            for start in starts:
                rows = slice(start, start + BLOCK)
                pre = (
                    dot(ring_rows(feature_ref, start - shift, BLOCK), conv_ref[0])
                    + dot(feature_ref[rows, :], conv_ref[1])
                    + dot(ring_rows(feature_ref, start + shift, BLOCK), conv_ref[2])
                )
                activ, slope = gelu_parts(pre)
                activ_ref[rows, :] = activ
                slope_ref[rows, :] = slope
                after = source[rows, :].astype(F32) + dot(activ, proj_ref[...])
                after = after.astype(BF)
                if b == 0:
                    mid_ref[rows, :] = after
                    enter(1, start, after.astype(F32))
                else:
                    out.source[rows, :] = after
            for result in saved[0][2:] + saved[1][:2] if b == 0 else [*saved[1][2:], out]:
                result.send()

    outs = staged_call(
        body, "forward",
        [Plain(state, anywhere=True), Plain(order_of(chans))]
        + [Plain(x, b) for b in range(2) for x in (conv, proj)],
        [wide] + [wide, wide, thin, thin] * 2, [pltpu.VMEM((total, chans), BF)] * 3, 2,
    )
    return outs[0], (outs[1:5], outs[5:9])


def put_ring_rows(ref, start, columns, value):
    total, count = ref.shape[0], value.shape[0]
    start %= total
    first = min(count, total - start)
    ref[start : start + first, columns] = value[:first]
    if first < count:
        ref[: count - first, columns] = value[first:]


def pull(from_ref, proj_ref, slope_ref, taps_ref, shift):
    total, mids = slope_ref.shape
    for start in range(0, total, BLOCK):
        rows = slice(start, start + BLOCK)
        pulled = dot_t(from_ref[rows, :], proj_ref[...])
        e = (pulled * slope_ref[rows, :].astype(F32)).astype(BF)
        for k in range(3):
            columns = slice(k * mids, (k + 1) * mids)
            put_ring_rows(taps_ref, start + (k - 1) * shift, columns, e)


def grow(from_ref, taps_ref, flat_ref, slope_ref, out_ref):
    for start in range(0, from_ref.shape[0], BLOCK):
        rows = slice(start, start + BLOCK)
        summed = dot_t(taps_ref[rows, :], flat_ref[...])
        grown = from_ref[rows, :].astype(F32) + summed * slope_ref[rows, :].astype(F32)
        out_ref[rows, :] = grown.astype(BF)


def slot_of(place_ref, c, y, b):
    half, k = (c + place_ref[0]) % 2, (y + 4 - place_ref[1]) % 4
    early = (k >= 2) if b == 0 else (k == 1) | (k == 2)
    return half * 2 + jnp.where(early, 0, 1), jnp.where(k % 2 == 0, b, (k + 3) // 2)


def conv_terms(place_ref, feature_ref, taps_ref, part_ref, b):
    chans, wide = feature_ref.shape[1], taps_ref.shape[1]
    rows = chans // 8
    for c in range(2):
        half = slice(4 * c * rows, 4 * (c + 1) * rows)
        terms = dot_rows(feature_ref[:, half], taps_ref[...]).astype(BF)
        for y in range(4):
            group, slot = slot_of(place_ref, c, y, b)
            part_ref[group, slot, :, :wide] = terms[y * rows : (y + 1) * rows]


def proj_terms(place_ref, grad_ref, activ_ref, part_ref, b, sum_ref, order_ref):
    chans, wide = grad_ref.shape[1], activ_ref.shape[1]
    share = chans // 128
    sum_ref[...] = dot_rows(grad_ref[...], activ_ref[...])
    for c in range(2):
        for y in range(4):
            ordered = order_ref.at[c * 4 + y]
            for q in range(16):
                owner = owner_of(c, y, q)
                ordered[q * share : (q + 1) * share, :] = sum_ref[
                    owner * share : (owner + 1) * share, :
                ]
            group, slot = slot_of(place_ref, c, y, b)
            part_ref[group, slot, :, 3 * wide :] = ordered[...].astype(BF)


def backward(grad, saved, conv, proj, step, place):
    total, chans = grad.shape
    mids = conv.shape[-1]
    rows = 16 * (chans // 128)
    ins = [Plain(grad, anywhere=True)]
    for b in (1, 0):
        feature, slope_in, activ, slope = saved[b]
        ins += [Plain(proj, b), Plain(slope), Plain(feature), Plain(activ)]
        ins += [Flat(conv, b), Plain(slope_in)]

    def body(fetched, sent, place_ref, grown_ref, taps_ref, sum_ref, order_ref):
        (grad_ref,), queue = get_then(fetched[:1], []), fetched[1:]
        out, part = sent
        for b in (1, 0):
            mine, queue = queue[:6], queue[6:]
            out_ref = grown_ref if b == 1 else out.source
            proj_ref, slope_ref = get_then(mine[:2], mine[2:] if b == 1 else [])
            pull(grad_ref, proj_ref, slope_ref, taps_ref, step * 2**b)
            feature_ref, activ_ref = get_then(mine[2:4], [])
            conv_terms(place_ref, feature_ref, taps_ref, part.source, b)
            proj_terms(place_ref, grad_ref, activ_ref, part.source, b, sum_ref, order_ref)
            if b == 0:
                part.send()
            flat_ref, slope_in_ref = get_then(mine[4:], queue)
            grow(grad_ref, taps_ref, flat_ref, slope_in_ref, out_ref)
            grad_ref = out_ref
        out.send()

    return staged_call(
        body, "backward", ins, [((total, chans), None), ((4, 4, rows, 4 * mids), 4)],
        [
            pltpu.VMEM((total, chans), BF),
            pltpu.VMEM((total, 3 * mids), BF),
            pltpu.VMEM((chans, mids), F32),
            pltpu.VMEM((8, rows, mids), F32),
        ],
        3, place,
    )


def to_rings(block):
    return lax.all_to_all(block, RING, 0, 0, tiled=True)


def passed(block, axis, distance):
    size = lax.axis_size(axis)
    return lax.ppermute(block, axis, [(i, (i + distance) % size) for i in range(size)])


def total_of(parts):
    out = parts[0].astype(F32)
    for part in parts[1:]:
        out = out + part.astype(F32)
    return out


def core_sum(mine, came):
    return [total_of([mine[i], came[i]]).astype(BF) for i in range(4)]


def column_sum(first, second, beside):
    two0, two1, right1, left0 = first
    own0, own1, right0, left1 = second
    two0, two1 = passed(two0, COLUMN, 1), passed(two1, COLUMN, -1)
    right1, left0 = passed(right1, COLUMN, 1), passed(left0, COLUMN, -1)
    right0 = passed(total_of([right0, two0]).astype(BF), COLUMN, 1)
    left1 = passed(total_of([left1, two1]).astype(BF), COLUMN, -1)
    right0, left1, beside = lax.optimization_barrier((right0, left1, beside))
    sums = total_of([own0, left0, right0]), total_of([own1, right1, left1])
    return jnp.stack(sums).astype(BF), beside


def ring_step(rows, second):
    pieces = rows.reshape(2, 4, -1, rows.shape[-1])
    x, z, c = (lax.axis_index(axis) for axis in ("x", "z", "c"))
    me = jnp.where(c == second, x, z)

    def piece(k):
        return lax.dynamic_index_in_dim(pieces, (me + k) % 4, 1, keepdims=False)

    def sent(k):
        route = []
        for i in range(32):
            x, z, c = i // 8, i // 2 % 4, i % 2
            x, z = ((x + k) % 4, z) if c == second else (x, (z + k) % 4)
            route.append((i, (x * 4 + z) * 2 + c))
        return lax.ppermute(piece(k), ("x", "z", "c"), route)

    return total_of([piece(0)] + [sent(k) for k in (2, 1, 3)])


def local(inputs, cotangent, conv, proj):
    genomes, bins, chans = inputs.shape
    total = genomes * bins
    step = total // 16
    mids = conv.shape[-1]

    def rings(block):
        return to_rings(block.reshape(16, step, chans)).reshape(total, chans)

    def unring(block):
        return to_rings(block.reshape(16, step, chans)).reshape(genomes, bins, chans)

    place = [lax.axis_index("c"), lax.axis_index(COLUMN)]
    place = jnp.stack(place).astype(jnp.int32)
    state = rings(inputs)
    grad = rings(cotangent)
    out, saved = forward(state, conv, proj, step)
    outputs = unring(out)
    grad, *parts = backward(grad, saved, conv, proj, step, place)
    input_grad = unring(grad)
    came = [passed(part, "c", 1) for part in parts[2:]]
    *came, outputs = lax.optimization_barrier((*came, outputs))
    first, second = core_sum(parts[0], came[0]), core_sum(parts[1], came[1])
    share, input_grad = column_sum(first, second, input_grad)
    share = ring_step(share, 0).astype(BF)
    outputs, input_grad = settled(outputs), settled(input_grad)
    share, outputs, input_grad = lax.optimization_barrier((share, outputs, input_grad))
    share = ring_step(share, 1) * jnp.float32(1.0 / math.sqrt(total * 128))
    share = share.reshape(2, -1, 4, mids)
    conv_out = share[:, :, :3].transpose(0, 2, 1, 3)
    proj_out = share[:, :, 3].transpose(0, 2, 1)
    return outputs, input_grad, conv_out, proj_out


def solution(mesh):
    fine = Mesh(mesh.devices.reshape(4, 4, 2, 2, 2), ("x", "z", "yh", "c", "yl"))
    rows = P("yl", SEQ, None)
    in_specs = (rows, rows, P(), P())
    out_specs = (rows, rows, P(None, None, SEQ + ("yl",), None), P(None, None, SEQ + ("yl",)))
    return jax.shard_map(local, mesh=fine, in_specs=in_specs, out_specs=out_specs, check_vma=False)
```

```python
import functools
import math

import jax
import jax.numpy as jnp
import numpy as np
from jax import lax
from jax.experimental import pallas as pl
from jax.experimental.pallas import tpu as pltpu
from jax.sharding import Mesh
from jax.sharding import PartitionSpec as P

RING = ("x", "z")
COLUMN = ("yh", "yl")
SEQ = ("x", "z", "yh", "c")
BF = jnp.bfloat16
F32 = jnp.float32
BLOCK = 256
VMEM_BYTES = 52 * 1024 * 1024


def gelu_parts(value):
    cdf = 0.5 * (1.0 + lax.erf(value * (1.0 / math.sqrt(2.0))))
    density = jnp.exp(-0.5 * value * value) * (1.0 / math.sqrt(2.0 * math.pi))
    return (value * cdf).astype(BF), (cdf + value * density).astype(BF)


def dot(left, right):
    return jnp.dot(left, right, preferred_element_type=F32)


def dot_t(left, right):
    return lax.dot_general(left, right, (((1,), (1,)), ((), ())), preferred_element_type=F32)


def dot_rows(left, right):
    return lax.dot_general(left, right, (((0,), (0,)), ((), ())), preferred_element_type=F32)


def ring_rows(ref, start, count):
    total = ref.shape[0]
    start %= total
    if start + count <= total:
        return ref[start : start + count, :]
    first = total - start
    return jnp.concatenate([ref[start:total, :], ref[: count - first, :]], axis=0)


class Fetched:
    def __init__(self, copies, target):
        self.copies, self.target, self.here = copies, target, False

    def start(self):
        for copy in self.copies:
            copy.start()

    def get(self):
        if not self.here:
            for copy in self.copies:
                copy.wait()
            self.here = True
        return self.target


class Sent:
    def __init__(self, source, copies):
        self.source, self.copies = source, copies

    def send(self):
        for copy in self.copies:
            copy.start()

    def finish(self):
        for copy in self.copies:
            copy.wait()


def get_then(wanted, following):
    refs = [f.get() for f in wanted]
    for f in following:
        f.start()
    return refs


class Flat:
    def __init__(self, array, b):
        self.array, self.b = array, b
        taps, chans, mids = array.shape[1:]
        self.shape = (chans, taps * mids)

    def copies(self, source, target, sems):
        mids = self.array.shape[-1]
        return [
            pltpu.make_async_copy(
                source.at[self.b, k], target.at[:, k * mids : (k + 1) * mids], sems.at[k]
            )
            for k in range(3)
        ]


class Plain:
    def __init__(self, array, b=None, anywhere=False):
        self.array, self.b, self.anywhere = array, b, anywhere
        self.shape = array.shape if b is None else array.shape[1:]

    def copies(self, source, target, sems):
        source = source if self.b is None else source.at[self.b]
        return [pltpu.make_async_copy(source, target, sems.at[0])]


def staged_call(body, name, ins, outs, scratch, urgent, place=None):
    kept_outs = [pltpu.VMEM(shape, BF) for shape, _ in outs]
    held = [pltpu.VMEM(x.shape, BF) for x in ins] + kept_outs
    results = [(i, k) for i, (_, count) in enumerate(outs) for k in range(count or 1)]
    n, m, held_n = len(ins), len(results), len(held)
    extra = [] if place is None else [place]

    def kernel(*refs):
        head, refs = refs[: len(extra)], refs[len(extra) :]
        sources, targets, kept = refs[:n], refs[n : n + m], refs[n + m : n + m + held_n]
        in_sems, out_sems = refs[n + m + held_n], refs[n + m + held_n + 1]
        rest = refs[n + m + held_n + 2 :]
        fetched = [
            Fetched(x.copies(sources[i], kept[i], in_sems.at[i]), kept[i])
            for i, x in enumerate(ins)
        ]
        for f in fetched[:urgent]:
            f.start()
        sent = [Sent(kept[n + i], []) for i in range(len(outs))]
        for j, (i, k) in enumerate(results):
            source = kept[n + i] if outs[i][1] is None else kept[n + i].at[k]
            sent[i].copies.append(pltpu.make_async_copy(source, targets[j], out_sems.at[j]))
        body(fetched, sent, *head, *rest)
        for result in sent:
            result.finish()

    def out_shape(i):
        shape, count = outs[i]
        return pltpu.HBM(shape if count is None else shape[1:], BF)

    return pl.pallas_call(
        kernel,
        out_shape=[out_shape(i) for i, _ in results],
        in_specs=[pl.BlockSpec(memory_space=pltpu.SMEM)] * len(extra)
        + [pl.BlockSpec(memory_space=pl.ANY if anywhere(x) else pltpu.HBM) for x in ins],
        out_specs=[pl.BlockSpec(memory_space=pltpu.HBM)] * m,
        scratch_shapes=held
        + [pltpu.SemaphoreType.DMA((n, 3)), pltpu.SemaphoreType.DMA((m,))]
        + list(scratch),
        compiler_params=pltpu.CompilerParams(vmem_limit_bytes=VMEM_BYTES),
        cost_estimate=pl.CostEstimate(flops=1, bytes_accessed=1, transcendentals=0),
        name=name,
    )(
        *extra,
        *[
            x.array if anywhere(x) else pltpu.with_memory_space_constraint(x.array, pltpu.HBM)
            for x in ins
        ],
    )


def anywhere(operand):
    return getattr(operand, "anywhere", False)


def settled(array):
    return array * lax.optimization_barrier(jnp.ones((), array.dtype))


def owner_of(c, y, q):
    ring = q if c == 0 else q % 4 * 4 + q // 4
    return ((ring * 2 + y // 2) * 2 + c) * 2 + y % 2


def order_of(chans):
    share = chans // 128
    owners = [owner_of(c, y, q) for c in range(2) for y in range(4) for q in range(16)]
    source = np.repeat(np.array(owners) * share, share) + np.tile(np.arange(share), 128)
    return jnp.asarray(np.arange(chans)[:, None] == source[None, :], BF)


def forward(state, conv, proj, step):
    total, chans = state.shape
    mids = conv.shape[-1]
    wide, thin = ((total, chans), None), ((total, mids), None)
    starts = range(0, total, BLOCK)

    def body(fetched, sent, mid_ref, *feature_refs):
        out, saved = sent[0], (sent[1:5], sent[5:9])

        def enter(b, start, value):
            rows = slice(start, start + BLOCK)
            feature, slope = gelu_parts(value)
            feature_refs[b][rows, :] = feature
            saved[b][0].source[rows, :] = dot(feature, order_ref[...]).astype(BF)
            saved[b][1].source[rows, :] = slope

        x_ref, order_ref = get_then(fetched[:2], fetched[2:])
        for start in starts:
            enter(0, start, x_ref[start : start + BLOCK, :].astype(F32))
        saved[0][0].send()
        saved[0][1].send()
        for b in range(2):
            feature_ref = feature_refs[b]
            activ_ref, slope_ref = saved[b][2].source, saved[b][3].source
            conv_ref, proj_ref = (f.get() for f in fetched[2 + 2 * b : 4 + 2 * b])
            source = x_ref if b == 0 else mid_ref
            shift = step * 2**b
            for start in starts:
                rows = slice(start, start + BLOCK)
                pre = (
                    dot(ring_rows(feature_ref, start - shift, BLOCK), conv_ref[0])
                    + dot(feature_ref[rows, :], conv_ref[1])
                    + dot(ring_rows(feature_ref, start + shift, BLOCK), conv_ref[2])
                )
                activ, slope = gelu_parts(pre)
                activ_ref[rows, :] = activ
                slope_ref[rows, :] = slope
                after = source[rows, :].astype(F32) + dot(activ, proj_ref[...])
                after = after.astype(BF)
                if b == 0:
                    mid_ref[rows, :] = after
                    enter(1, start, after.astype(F32))
                else:
                    out.source[rows, :] = after
            for result in saved[0][2:] + saved[1][:2] if b == 0 else [*saved[1][2:], out]:
                result.send()

    outs = staged_call(
        body, "forward",
        [Plain(state, anywhere=True), Plain(order_of(chans))]
        + [Plain(x, b) for b in range(2) for x in (conv, proj)],
        [wide] + [wide, wide, thin, thin] * 2, [pltpu.VMEM((total, chans), BF)] * 3, 2,
    )
    return outs[0], (outs[1:5], outs[5:9])


def put_ring_rows(ref, start, columns, value):
    total, count = ref.shape[0], value.shape[0]
    start %= total
    first = min(count, total - start)
    ref[start : start + first, columns] = value[:first]
    if first < count:
        ref[: count - first, columns] = value[first:]


def pull(from_ref, proj_ref, slope_ref, taps_ref, shift):
    total, mids = slope_ref.shape
    for start in range(0, total, BLOCK):
        rows = slice(start, start + BLOCK)
        pulled = dot_t(from_ref[rows, :], proj_ref[...])
        e = (pulled * slope_ref[rows, :].astype(F32)).astype(BF)
        for k in range(3):
            columns = slice(k * mids, (k + 1) * mids)
            put_ring_rows(taps_ref, start + (k - 1) * shift, columns, e)


def grow(from_ref, taps_ref, flat_ref, slope_ref, out_ref):
    for start in range(0, from_ref.shape[0], BLOCK):
        rows = slice(start, start + BLOCK)
        summed = dot_t(taps_ref[rows, :], flat_ref[...])
        grown = from_ref[rows, :].astype(F32) + summed * slope_ref[rows, :].astype(F32)
        out_ref[rows, :] = grown.astype(BF)


def slot_of(place_ref, c, y, b):
    half, k = (c + place_ref[0]) % 2, (y + 4 - place_ref[1]) % 4
    early = (k >= 2) if b == 0 else (k == 1) | (k == 2)
    return half * 2 + jnp.where(early, 0, 1), jnp.where(k % 2 == 0, b, (k + 3) // 2)


def conv_terms(place_ref, feature_ref, taps_ref, part_ref, b):
    chans, wide = feature_ref.shape[1], taps_ref.shape[1]
    rows = chans // 8
    for c in range(2):
        half = slice(4 * c * rows, 4 * (c + 1) * rows)
        terms = dot_rows(feature_ref[:, half], taps_ref[...]).astype(BF)
        for y in range(4):
            group, slot = slot_of(place_ref, c, y, b)
            part_ref[group, slot, :, :wide] = terms[y * rows : (y + 1) * rows]


def proj_terms(place_ref, grad_ref, activ_ref, part_ref, b, sum_ref, order_ref):
    chans, wide = grad_ref.shape[1], activ_ref.shape[1]
    share = chans // 128
    sum_ref[...] = dot_rows(grad_ref[...], activ_ref[...])
    for c in range(2):
        for y in range(4):
            ordered = order_ref.at[c * 4 + y]
            for q in range(16):
                owner = owner_of(c, y, q)
                ordered[q * share : (q + 1) * share, :] = sum_ref[
                    owner * share : (owner + 1) * share, :
                ]
            group, slot = slot_of(place_ref, c, y, b)
            part_ref[group, slot, :, 3 * wide :] = ordered[...].astype(BF)


def backward(grad, saved, conv, proj, step, place):
    total, chans = grad.shape
    mids = conv.shape[-1]
    rows = 16 * (chans // 128)
    ins = [Plain(grad, anywhere=True)]
    for b in (1, 0):
        feature, slope_in, activ, slope = saved[b]
        ins += [Plain(proj, b), Plain(slope), Plain(feature), Plain(activ)]
        ins += [Flat(conv, b), Plain(slope_in)]

    def body(fetched, sent, place_ref, grown_ref, taps_ref, sum_ref, order_ref):
        (grad_ref,), queue = get_then(fetched[:1], []), fetched[1:]
        out, part = sent
        for b in (1, 0):
            mine, queue = queue[:6], queue[6:]
            out_ref = grown_ref if b == 1 else out.source
            proj_ref, slope_ref = get_then(mine[:2], mine[2:] if b == 1 else [])
            pull(grad_ref, proj_ref, slope_ref, taps_ref, step * 2**b)
            feature_ref, activ_ref = get_then(mine[2:4], [])
            conv_terms(place_ref, feature_ref, taps_ref, part.source, b)
            proj_terms(place_ref, grad_ref, activ_ref, part.source, b, sum_ref, order_ref)
            if b == 0:
                part.send()
            flat_ref, slope_in_ref = get_then(mine[4:], queue)
            grow(grad_ref, taps_ref, flat_ref, slope_in_ref, out_ref)
            grad_ref = out_ref
        out.send()

    return staged_call(
        body, "backward", ins, [((total, chans), None), ((4, 4, rows, 4 * mids), 4)],
        [
            pltpu.VMEM((total, chans), BF),
            pltpu.VMEM((total, 3 * mids), BF),
            pltpu.VMEM((chans, mids), F32),
            pltpu.VMEM((8, rows, mids), F32),
        ],
        3, place,
    )


def to_rings(block):
    return lax.all_to_all(block, RING, 0, 0, tiled=True)


def passed(block, axis, distance):
    size = lax.axis_size(axis)
    return lax.ppermute(block, axis, [(i, (i + distance) % size) for i in range(size)])


def total_of(parts):
    out = parts[0].astype(F32)
    for part in parts[1:]:
        out = out + part.astype(F32)
    return out


def core_sum(mine, came, *at):
    return [total_of([mine[i], came[i]]).astype(BF) for i in at]


def column_sum(first, second, beside):
    two0, two1, right1, left0 = first
    own, right0, left1 = second
    two0, two1 = passed(two0, COLUMN, 1), passed(two1, COLUMN, -1)
    right1, left0 = passed(right1, COLUMN, 1), passed(left0, COLUMN, -1)
    right0 = passed(total_of([right0, two0]).astype(BF), COLUMN, 1)
    left1 = passed(total_of([left1, two1]).astype(BF), COLUMN, -1)
    right0, left1, beside = lax.optimization_barrier((right0, left1, beside))
    return total_of([own, jnp.stack([left0, right1]), jnp.stack([right0, left1])]).astype(BF), beside


def ring_step(rows, second):
    pieces = rows.reshape(2, 4, -1, rows.shape[-1])
    x, z, c = (lax.axis_index(axis) for axis in ("x", "z", "c"))
    me = jnp.where(c == second, x, z)

    def piece(k):
        return lax.dynamic_index_in_dim(pieces, (me + k) % 4, 1, keepdims=False)

    def sent(k):
        route = []
        for i in range(32):
            x, z, c = i // 8, i // 2 % 4, i % 2
            x, z = ((x + k) % 4, z) if c == second else (x, (z + k) % 4)
            route.append((i, (x * 4 + z) * 2 + c))
        return lax.ppermute(piece(k), ("x", "z", "c"), route)

    return total_of([piece(0)] + [sent(k) for k in (2, 1, 3)])


def local(inputs, cotangent, conv, proj):
    genomes, bins, chans = inputs.shape
    total = genomes * bins
    step = total // 16
    mids = conv.shape[-1]

    def rings(block):
        return to_rings(block.reshape(16, step, chans)).reshape(total, chans)

    def unring(block):
        return to_rings(block.reshape(16, step, chans)).reshape(genomes, bins, chans)

    place = [lax.axis_index("c"), lax.axis_index(COLUMN)]
    place = jnp.stack(place).astype(jnp.int32)
    state = rings(inputs)
    grad = rings(cotangent)
    out, saved = forward(state, conv, proj, step)
    outputs = unring(out)
    grad, *parts = backward(grad, saved, conv, proj, step, place)
    input_grad = unring(grad)
    came = [passed(part, "c", 1) for part in parts[2:]]
    *came, outputs = lax.optimization_barrier((*came, outputs))
    first = core_sum(parts[0], came[0], 0, 1, 2, 3)
    second = core_sum(parts[1], came[1], slice(2), 2, 3)
    share, input_grad = column_sum(first, second, input_grad)
    share = ring_step(share, 0).astype(BF)
    outputs, input_grad = settled(outputs), settled(input_grad)
    share, outputs, input_grad = lax.optimization_barrier((share, outputs, input_grad))
    share = ring_step(share, 1) * jnp.float32(1.0 / math.sqrt(total * 128))
    share = share.reshape(2, -1, 4, mids)
    conv_out = share[:, :, :3].transpose(0, 2, 1, 3)
    proj_out = share[:, :, 3].transpose(0, 2, 1)
    return outputs, input_grad, conv_out, proj_out


def solution(mesh):
    fine = Mesh(mesh.devices.reshape(4, 4, 2, 2, 2), ("x", "z", "yh", "c", "yl"))
    rows = P("yl", SEQ, None)
    in_specs = (rows, rows, P(), P())
    out_specs = (rows, rows, P(None, None, SEQ + ("yl",), None), P(None, None, SEQ + ("yl",)))
    return jax.shard_map(local, mesh=fine, in_specs=in_specs, out_specs=out_specs, check_vma=False)
```

```python
import functools
import math

import jax
import jax.numpy as jnp
import numpy as np
from jax import lax
from jax.experimental import pallas as pl
from jax.experimental.pallas import tpu as pltpu
from jax.sharding import Mesh
from jax.sharding import PartitionSpec as P

RING = ("x", "z")
COLUMN = ("yh", "yl")
SEQ = ("x", "z", "yh", "c")
BF = jnp.bfloat16
F32 = jnp.float32
BLOCK = 256
VMEM_BYTES = 52 * 1024 * 1024


def gelu_parts(value):
    cdf = 0.5 * (1.0 + lax.erf(value * (1.0 / math.sqrt(2.0))))
    density = jnp.exp(-0.5 * value * value) * (1.0 / math.sqrt(2.0 * math.pi))
    return (value * cdf).astype(BF), (cdf + value * density).astype(BF)


def dot(left, right):
    return jnp.dot(left, right, preferred_element_type=F32)


def dot_t(left, right):
    return lax.dot_general(left, right, (((1,), (1,)), ((), ())), preferred_element_type=F32)


def dot_rows(left, right):
    return lax.dot_general(left, right, (((0,), (0,)), ((), ())), preferred_element_type=F32)


def ring_rows(ref, start, count):
    total = ref.shape[0]
    start %= total
    if start + count <= total:
        return ref[start : start + count, :]
    first = total - start
    return jnp.concatenate([ref[start:total, :], ref[: count - first, :]], axis=0)


class Fetched:
    def __init__(self, copies, target):
        self.copies, self.target, self.here = copies, target, False

    def start(self):
        for copy in self.copies:
            copy.start()

    def get(self):
        if not self.here:
            for copy in self.copies:
                copy.wait()
            self.here = True
        return self.target


class Sent:
    def __init__(self, source, copies):
        self.source, self.copies = source, copies

    def send(self):
        for copy in self.copies:
            copy.start()

    def finish(self):
        for copy in self.copies:
            copy.wait()


def get_then(wanted, following):
    refs = [f.get() for f in wanted]
    for f in following:
        f.start()
    return refs


class Flat:
    def __init__(self, array, b):
        self.array, self.b = array, b
        taps, chans, mids = array.shape[1:]
        self.shape = (chans, taps * mids)

    def copies(self, source, target, sems):
        mids = self.array.shape[-1]
        return [
            pltpu.make_async_copy(
                source.at[self.b, k], target.at[:, k * mids : (k + 1) * mids], sems.at[k]
            )
            for k in range(3)
        ]


class Plain:
    def __init__(self, array, b=None, anywhere=False):
        self.array, self.b, self.anywhere = array, b, anywhere
        self.shape = array.shape if b is None else array.shape[1:]

    def copies(self, source, target, sems):
        source = source if self.b is None else source.at[self.b]
        return [pltpu.make_async_copy(source, target, sems.at[0])]


def staged_call(body, name, ins, outs, scratch, urgent, place=None):
    kept_outs = [pltpu.VMEM(shape, BF) for shape, _ in outs]
    held = [pltpu.VMEM(x.shape, BF) for x in ins] + kept_outs
    results = [(i, k) for i, (_, count) in enumerate(outs) for k in range(count or 1)]
    n, m, held_n = len(ins), len(results), len(held)
    extra = [] if place is None else [place]

    def kernel(*refs):
        head, refs = refs[: len(extra)], refs[len(extra) :]
        sources, targets, kept = refs[:n], refs[n : n + m], refs[n + m : n + m + held_n]
        in_sems, out_sems = refs[n + m + held_n], refs[n + m + held_n + 1]
        rest = refs[n + m + held_n + 2 :]
        fetched = [
            Fetched(x.copies(sources[i], kept[i], in_sems.at[i]), kept[i])
            for i, x in enumerate(ins)
        ]
        for f in fetched[:urgent]:
            f.start()
        sent = [Sent(kept[n + i], []) for i in range(len(outs))]
        for j, (i, k) in enumerate(results):
            source = kept[n + i] if outs[i][1] is None else kept[n + i].at[k]
            sent[i].copies.append(pltpu.make_async_copy(source, targets[j], out_sems.at[j]))
        body(fetched, sent, *head, *rest)
        for result in sent:
            result.finish()

    def out_shape(i):
        shape, count = outs[i]
        return pltpu.HBM(shape if count is None else shape[1:], BF)

    return pl.pallas_call(
        kernel,
        out_shape=[out_shape(i) for i, _ in results],
        in_specs=[pl.BlockSpec(memory_space=pltpu.SMEM)] * len(extra)
        + [pl.BlockSpec(memory_space=pl.ANY if anywhere(x) else pltpu.HBM) for x in ins],
        out_specs=[pl.BlockSpec(memory_space=pltpu.HBM)] * m,
        scratch_shapes=held
        + [pltpu.SemaphoreType.DMA((n, 3)), pltpu.SemaphoreType.DMA((m,))]
        + list(scratch),
        compiler_params=pltpu.CompilerParams(vmem_limit_bytes=VMEM_BYTES),
        cost_estimate=pl.CostEstimate(flops=1, bytes_accessed=1, transcendentals=0),
        name=name,
    )(
        *extra,
        *[
            x.array if anywhere(x) else pltpu.with_memory_space_constraint(x.array, pltpu.HBM)
            for x in ins
        ],
    )


def anywhere(operand):
    return getattr(operand, "anywhere", False)


def settled(array):
    return array * lax.optimization_barrier(jnp.ones((), array.dtype))


def owner_of(c, y, q):
    ring = q if c == 0 else q % 4 * 4 + q // 4
    return ((ring * 2 + y // 2) * 2 + c) * 2 + y % 2


def order_of(chans):
    share = chans // 128
    owners = [owner_of(c, y, q) for c in range(2) for y in range(4) for q in range(16)]
    source = np.repeat(np.array(owners) * share, share) + np.tile(np.arange(share), 128)
    return jnp.asarray(np.arange(chans)[:, None] == source[None, :], BF)


def forward(state, conv, proj, step):
    total, chans = state.shape
    mids = conv.shape[-1]
    wide, thin = ((total, chans), None), ((total, mids), None)
    starts = range(0, total, BLOCK)

    def body(fetched, sent, mid_ref, *feature_refs):
        out, saved = sent[0], (sent[1:5], sent[5:9])

        def enter(b, start, value):
            rows = slice(start, start + BLOCK)
            feature, slope = gelu_parts(value)
            feature_refs[b][rows, :] = feature
            saved[b][0].source[rows, :] = dot(feature, order_ref[...]).astype(BF)
            saved[b][1].source[rows, :] = slope

        x_ref, order_ref = get_then(fetched[:2], fetched[2:])
        for start in starts:
            enter(0, start, x_ref[start : start + BLOCK, :].astype(F32))
        saved[0][0].send()
        saved[0][1].send()
        for b in range(2):
            feature_ref = feature_refs[b]
            activ_ref, slope_ref = saved[b][2].source, saved[b][3].source
            conv_ref, proj_ref = (f.get() for f in fetched[2 + 2 * b : 4 + 2 * b])
            source = x_ref if b == 0 else mid_ref
            shift = step * 2**b
            for start in starts:
                rows = slice(start, start + BLOCK)
                pre = (
                    dot(ring_rows(feature_ref, start - shift, BLOCK), conv_ref[0])
                    + dot(feature_ref[rows, :], conv_ref[1])
                    + dot(ring_rows(feature_ref, start + shift, BLOCK), conv_ref[2])
                )
                activ, slope = gelu_parts(pre)
                activ_ref[rows, :] = activ
                slope_ref[rows, :] = slope
                after = source[rows, :].astype(F32) + dot(activ, proj_ref[...])
                after = after.astype(BF)
                if b == 0:
                    mid_ref[rows, :] = after
                    enter(1, start, after.astype(F32))
                else:
                    out.source[rows, :] = after
            for result in saved[0][2:] + saved[1][:2] if b == 0 else [*saved[1][2:], out]:
                result.send()

    outs = staged_call(
        body, "forward",
        [Plain(state, anywhere=True), Plain(order_of(chans))]
        + [Plain(x, b) for b in range(2) for x in (conv, proj)],
        [wide] + [wide, wide, thin, thin] * 2, [pltpu.VMEM((total, chans), BF)] * 3, 2,
    )
    return outs[0], (outs[1:5], outs[5:9])


def put_ring_rows(ref, start, columns, value):
    total, count = ref.shape[0], value.shape[0]
    start %= total
    first = min(count, total - start)
    ref[start : start + first, columns] = value[:first]
    if first < count:
        ref[: count - first, columns] = value[first:]


def pull(from_ref, proj_ref, slope_ref, taps_ref, shift):
    total, mids = slope_ref.shape
    for start in range(0, total, BLOCK):
        rows = slice(start, start + BLOCK)
        pulled = dot_t(from_ref[rows, :], proj_ref[...])
        e = (pulled * slope_ref[rows, :].astype(F32)).astype(BF)
        for k in range(3):
            columns = slice(k * mids, (k + 1) * mids)
            put_ring_rows(taps_ref, start + (k - 1) * shift, columns, e)


def grow(from_ref, taps_ref, flat_ref, slope_ref, out_ref):
    for start in range(0, from_ref.shape[0], BLOCK):
        rows = slice(start, start + BLOCK)
        summed = dot_t(taps_ref[rows, :], flat_ref[...])
        grown = from_ref[rows, :].astype(F32) + summed * slope_ref[rows, :].astype(F32)
        out_ref[rows, :] = grown.astype(BF)


def slot_of(place_ref, c, y, b):
    half, k = (c + place_ref[0]) % 2, (y + 4 - place_ref[1]) % 4
    early = (k >= 2) if b == 0 else (k == 1) | (k == 2)
    return half * 2 + jnp.where(early, 0, 1), jnp.where(k % 2 == 0, b, (k + 3) // 2)


def conv_terms(place_ref, feature_ref, taps_ref, part_ref, b):
    chans, wide = feature_ref.shape[1], taps_ref.shape[1]
    rows = chans // 8
    for c in range(2):
        half = slice(4 * c * rows, 4 * (c + 1) * rows)
        terms = dot_rows(feature_ref[:, half], taps_ref[...]).astype(BF)
        for y in range(4):
            group, slot = slot_of(place_ref, c, y, b)
            part_ref[group, slot, :, :wide] = terms[y * rows : (y + 1) * rows]


def proj_terms(place_ref, grad_ref, activ_ref, part_ref, b, sum_ref, order_ref):
    chans, wide = grad_ref.shape[1], activ_ref.shape[1]
    share = chans // 128
    sum_ref[...] = dot_rows(grad_ref[...], activ_ref[...])
    for c in range(2):
        for y in range(4):
            ordered = order_ref.at[c * 4 + y]
            for q in range(16):
                owner = owner_of(c, y, q)
                ordered[q * share : (q + 1) * share, :] = sum_ref[
                    owner * share : (owner + 1) * share, :
                ]
            group, slot = slot_of(place_ref, c, y, b)
            part_ref[group, slot, :, 3 * wide :] = ordered[...].astype(BF)


def backward(grad, saved, conv, proj, step, place):
    total, chans = grad.shape
    mids = conv.shape[-1]
    rows = 16 * (chans // 128)
    ins = [Plain(grad, anywhere=True)]
    for b in (1, 0):
        feature, slope_in, activ, slope = saved[b]
        ins += [Plain(proj, b), Plain(slope), Plain(feature), Plain(activ)]
        ins += [Flat(conv, b), Plain(slope_in)]

    def body(fetched, sent, place_ref, grown_ref, taps_ref, sum_ref, order_ref):
        (grad_ref,), queue = get_then(fetched[:1], []), fetched[1:]
        out, part = sent
        for b in (1, 0):
            mine, queue = queue[:6], queue[6:]
            out_ref = grown_ref if b == 1 else out.source
            proj_ref, slope_ref = get_then(mine[:2], mine[2:] if b == 1 else [])
            pull(grad_ref, proj_ref, slope_ref, taps_ref, step * 2**b)
            feature_ref, activ_ref = get_then(mine[2:4], [])
            conv_terms(place_ref, feature_ref, taps_ref, part.source, b)
            proj_terms(place_ref, grad_ref, activ_ref, part.source, b, sum_ref, order_ref)
            if b == 0:
                part.send()
            flat_ref, slope_in_ref = get_then(mine[4:], queue)
            grow(grad_ref, taps_ref, flat_ref, slope_in_ref, out_ref)
            grad_ref = out_ref
        out.send()

    return staged_call(
        body, "backward", ins, [((total, chans), None), ((4, 4, rows, 4 * mids), 4)],
        [
            pltpu.VMEM((total, chans), BF),
            pltpu.VMEM((total, 3 * mids), BF),
            pltpu.VMEM((chans, mids), F32),
            pltpu.VMEM((8, rows, mids), F32),
        ],
        3, place,
    )


def to_rings(block):
    return lax.all_to_all(block, RING, 0, 0, tiled=True)


def passed(block, axis, distance):
    size = lax.axis_size(axis)
    return lax.ppermute(block, axis, [(i, (i + distance) % size) for i in range(size)])


def total_of(parts):
    out = parts[0].astype(F32)
    for part in parts[1:]:
        out = out + part.astype(F32)
    return out


def core_sum(mine, came, *at):
    return [total_of([mine[i], came[i]]).astype(BF) for i in at]


def column_sum(first, second, beside):
    two0, two1, right1, left0 = first
    own, right0, left1 = second
    two0, two1 = passed(two0, COLUMN, 1), passed(two1, COLUMN, -1)
    right1, left0 = passed(right1, COLUMN, 1), passed(left0, COLUMN, -1)
    right0 = passed(total_of([right0, two0]).astype(BF), COLUMN, 1)
    left1 = passed(total_of([left1, two1]).astype(BF), COLUMN, -1)
    right0, left1, beside = lax.optimization_barrier((right0, left1, beside))
    return total_of([own, jnp.stack([left0, right1]), jnp.stack([right0, left1])]).astype(BF), beside


def ring_step(rows, second):
    pieces = rows.reshape(2, 4, -1, rows.shape[-1])
    x, z, c = (lax.axis_index(axis) for axis in ("x", "z", "c"))
    me = jnp.where(c == second, x, z)

    def piece(k):
        return lax.dynamic_index_in_dim(pieces, (me + k) % 4, 1, keepdims=False)

    def sent(k):
        route = []
        for i in range(32):
            x, z, c = i // 8, i // 2 % 4, i % 2
            x, z = ((x + k) % 4, z) if c == second else (x, (z + k) % 4)
            route.append((i, (x * 4 + z) * 2 + c))
        return lax.ppermute(piece(k), ("x", "z", "c"), route)

    return total_of([piece(0)] + [sent(k) for k in (2, 1, 3)])


def local(inputs, cotangent, conv, proj):
    genomes, bins, chans = inputs.shape
    total = genomes * bins
    step = total // 16
    mids = conv.shape[-1]

    def rings(block):
        return to_rings(block.reshape(16, step, chans)).reshape(total, chans)

    def unring(block):
        return to_rings(block.reshape(16, step, chans)).reshape(genomes, bins, chans)

    place = [lax.axis_index("c"), lax.axis_index(COLUMN)]
    place = jnp.stack(place).astype(jnp.int32)
    state = rings(inputs)
    grad = rings(cotangent)
    out, saved = forward(state, conv, proj, step)
    outputs = unring(out)
    grad, *parts = backward(grad, saved, conv, proj, step, place)
    input_grad = unring(grad)
    came = [passed(part, "c", 1) for part in parts[2:]]
    *came, outputs = lax.optimization_barrier((*came, outputs))
    first = core_sum(parts[0], came[0], 0, 1)
    *first, rest = lax.optimization_barrier((*first, came[0]))
    first += core_sum(parts[0], rest, 2, 3)
    second = core_sum(parts[1], came[1], slice(2), 2, 3)
    share, input_grad = column_sum(first, second, input_grad)
    share = ring_step(share, 0).astype(BF)
    outputs, input_grad = settled(outputs), settled(input_grad)
    share, outputs, input_grad = lax.optimization_barrier((share, outputs, input_grad))
    share = ring_step(share, 1) * jnp.float32(1.0 / math.sqrt(total * 128))
    share = share.reshape(2, -1, 4, mids)
    conv_out = share[:, :, :3].transpose(0, 2, 1, 3)
    proj_out = share[:, :, 3].transpose(0, 2, 1)
    return outputs, input_grad, conv_out, proj_out


def solution(mesh):
    fine = Mesh(mesh.devices.reshape(4, 4, 2, 2, 2), ("x", "z", "yh", "c", "yl"))
    rows = P("yl", SEQ, None)
    in_specs = (rows, rows, P(), P())
    out_specs = (rows, rows, P(None, None, SEQ + ("yl",), None), P(None, None, SEQ + ("yl",)))
    return jax.shard_map(local, mesh=fine, in_specs=in_specs, out_specs=out_specs, check_vma=False)
```

```python
import functools
import math

import jax
import jax.numpy as jnp
import numpy as np
from jax import lax
from jax.experimental import pallas as pl
from jax.experimental.pallas import tpu as pltpu
from jax.sharding import Mesh
from jax.sharding import PartitionSpec as P

RING = ("x", "z")
COLUMN = ("yh", "yl")
SEQ = ("x", "z", "yh", "c")
BF = jnp.bfloat16
F32 = jnp.float32
BLOCK = 256
VMEM_BYTES = 52 * 1024 * 1024


def gelu_parts(value):
    cdf = 0.5 * (1.0 + lax.erf(value * (1.0 / math.sqrt(2.0))))
    density = jnp.exp(-0.5 * value * value) * (1.0 / math.sqrt(2.0 * math.pi))
    return (value * cdf).astype(BF), (cdf + value * density).astype(BF)


def dot(left, right):
    return jnp.dot(left, right, preferred_element_type=F32)


def dot_t(left, right):
    return lax.dot_general(left, right, (((1,), (1,)), ((), ())), preferred_element_type=F32)


def dot_rows(left, right):
    return lax.dot_general(left, right, (((0,), (0,)), ((), ())), preferred_element_type=F32)


def ring_rows(ref, start, count):
    total = ref.shape[0]
    start %= total
    if start + count <= total:
        return ref[start : start + count, :]
    first = total - start
    return jnp.concatenate([ref[start:total, :], ref[: count - first, :]], axis=0)


class Fetched:
    def __init__(self, copies, target):
        self.copies, self.target, self.here = copies, target, False

    def start(self):
        for copy in self.copies:
            copy.start()

    def get(self):
        if not self.here:
            for copy in self.copies:
                copy.wait()
            self.here = True
        return self.target


class Sent:
    def __init__(self, source, copies):
        self.source, self.copies = source, copies

    def send(self):
        for copy in self.copies:
            copy.start()

    def finish(self):
        for copy in self.copies:
            copy.wait()


def get_then(wanted, following):
    refs = [f.get() for f in wanted]
    for f in following:
        f.start()
    return refs


class Flat:
    def __init__(self, array, b):
        self.array, self.b = array, b
        taps, chans, mids = array.shape[1:]
        self.shape = (chans, taps * mids)

    def copies(self, source, target, sems):
        mids = self.array.shape[-1]
        return [
            pltpu.make_async_copy(
                source.at[self.b, k], target.at[:, k * mids : (k + 1) * mids], sems.at[k]
            )
            for k in range(3)
        ]


class Plain:
    def __init__(self, array, b=None, anywhere=False):
        self.array, self.b, self.anywhere = array, b, anywhere
        self.shape = array.shape if b is None else array.shape[1:]

    def copies(self, source, target, sems):
        source = source if self.b is None else source.at[self.b]
        return [pltpu.make_async_copy(source, target, sems.at[0])]


def staged_call(body, name, ins, outs, scratch, urgent, place=None):
    kept_outs = [pltpu.VMEM(shape, BF) for shape, _ in outs]
    held = [pltpu.VMEM(x.shape, BF) for x in ins] + kept_outs
    results = [(i, k) for i, (_, count) in enumerate(outs) for k in range(count or 1)]
    n, m, held_n = len(ins), len(results), len(held)
    extra = [] if place is None else [place]

    def kernel(*refs):
        head, refs = refs[: len(extra)], refs[len(extra) :]
        sources, targets, kept = refs[:n], refs[n : n + m], refs[n + m : n + m + held_n]
        in_sems, out_sems = refs[n + m + held_n], refs[n + m + held_n + 1]
        rest = refs[n + m + held_n + 2 :]
        fetched = [
            Fetched(x.copies(sources[i], kept[i], in_sems.at[i]), kept[i])
            for i, x in enumerate(ins)
        ]
        for f in fetched[:urgent]:
            f.start()
        sent = [Sent(kept[n + i], []) for i in range(len(outs))]
        for j, (i, k) in enumerate(results):
            source = kept[n + i] if outs[i][1] is None else kept[n + i].at[k]
            sent[i].copies.append(pltpu.make_async_copy(source, targets[j], out_sems.at[j]))
        body(fetched, sent, *head, *rest)
        for result in sent:
            result.finish()

    def out_shape(i):
        shape, count = outs[i]
        return pltpu.HBM(shape if count is None else shape[1:], BF)

    return pl.pallas_call(
        kernel,
        out_shape=[out_shape(i) for i, _ in results],
        in_specs=[pl.BlockSpec(memory_space=pltpu.SMEM)] * len(extra)
        + [pl.BlockSpec(memory_space=pl.ANY if anywhere(x) else pltpu.HBM) for x in ins],
        out_specs=[pl.BlockSpec(memory_space=pltpu.HBM)] * m,
        scratch_shapes=held
        + [pltpu.SemaphoreType.DMA((n, 3)), pltpu.SemaphoreType.DMA((m,))]
        + list(scratch),
        compiler_params=pltpu.CompilerParams(vmem_limit_bytes=VMEM_BYTES),
        cost_estimate=pl.CostEstimate(flops=1, bytes_accessed=1, transcendentals=0),
        name=name,
    )(
        *extra,
        *[
            x.array if anywhere(x) else pltpu.with_memory_space_constraint(x.array, pltpu.HBM)
            for x in ins
        ],
    )


def anywhere(operand):
    return getattr(operand, "anywhere", False)


def settled(array):
    return array * lax.optimization_barrier(jnp.ones((), array.dtype))


def owner_of(c, y, q):
    ring = q if c == 0 else q % 4 * 4 + q // 4
    return ((ring * 2 + y // 2) * 2 + c) * 2 + y % 2


def order_of(chans):
    share = chans // 128
    owners = [owner_of(c, y, q) for c in range(2) for y in range(4) for q in range(16)]
    source = np.repeat(np.array(owners) * share, share) + np.tile(np.arange(share), 128)
    return jnp.asarray(np.arange(chans)[:, None] == source[None, :], BF)


def forward(state, conv, proj, step):
    total, chans = state.shape
    mids = conv.shape[-1]
    wide, thin = ((total, chans), None), ((total, mids), None)
    starts = range(0, total, BLOCK)

    def body(fetched, sent, mid_ref, *feature_refs):
        out, saved = sent[0], (sent[1:5], sent[5:9])

        def enter(b, start, value):
            rows = slice(start, start + BLOCK)
            feature, slope = gelu_parts(value)
            feature_refs[b][rows, :] = feature
            saved[b][0].source[rows, :] = dot(feature, order_ref[...]).astype(BF)
            saved[b][1].source[rows, :] = slope

        x_ref, order_ref = get_then(fetched[:2], fetched[2:])
        for start in starts:
            enter(0, start, x_ref[start : start + BLOCK, :].astype(F32))
        saved[0][0].send()
        saved[0][1].send()
        for b in range(2):
            feature_ref = feature_refs[b]
            activ_ref, slope_ref = saved[b][2].source, saved[b][3].source
            conv_ref, proj_ref = (f.get() for f in fetched[2 + 2 * b : 4 + 2 * b])
            source = x_ref if b == 0 else mid_ref
            shift = step * 2**b
            for start in starts:
                rows = slice(start, start + BLOCK)
                pre = (
                    dot(ring_rows(feature_ref, start - shift, BLOCK), conv_ref[0])
                    + dot(feature_ref[rows, :], conv_ref[1])
                    + dot(ring_rows(feature_ref, start + shift, BLOCK), conv_ref[2])
                )
                activ, slope = gelu_parts(pre)
                activ_ref[rows, :] = activ
                slope_ref[rows, :] = slope
                after = source[rows, :].astype(F32) + dot(activ, proj_ref[...])
                after = after.astype(BF)
                if b == 0:
                    mid_ref[rows, :] = after
                    enter(1, start, after.astype(F32))
                else:
                    out.source[rows, :] = after
            for result in saved[0][2:] + saved[1][:2] if b == 0 else [*saved[1][2:], out]:
                result.send()

    outs = staged_call(
        body, "forward",
        [Plain(state, anywhere=True), Plain(order_of(chans))]
        + [Plain(x, b) for b in range(2) for x in (conv, proj)],
        [wide] + [wide, wide, thin, thin] * 2, [pltpu.VMEM((total, chans), BF)] * 3, 2,
    )
    return outs[0], (outs[1:5], outs[5:9])


def put_ring_rows(ref, start, columns, value):
    total, count = ref.shape[0], value.shape[0]
    start %= total
    first = min(count, total - start)
    ref[start : start + first, columns] = value[:first]
    if first < count:
        ref[: count - first, columns] = value[first:]


def pull(from_ref, proj_ref, slope_ref, taps_ref, shift):
    total, mids = slope_ref.shape
    for start in range(0, total, BLOCK):
        rows = slice(start, start + BLOCK)
        pulled = dot_t(from_ref[rows, :], proj_ref[...])
        e = (pulled * slope_ref[rows, :].astype(F32)).astype(BF)
        for k in range(3):
            columns = slice(k * mids, (k + 1) * mids)
            put_ring_rows(taps_ref, start + (k - 1) * shift, columns, e)


def grow(from_ref, taps_ref, flat_ref, slope_ref, out_ref):
    for start in range(0, from_ref.shape[0], BLOCK):
        rows = slice(start, start + BLOCK)
        summed = dot_t(taps_ref[rows, :], flat_ref[...])
        grown = from_ref[rows, :].astype(F32) + summed * slope_ref[rows, :].astype(F32)
        out_ref[rows, :] = grown.astype(BF)


def slot_of(place_ref, c, y, b):
    half, k = (c + place_ref[0]) % 2, (y + 4 - place_ref[1]) % 4
    early = (k >= 2) if b == 0 else (k == 1) | (k == 2)
    return half * 2 + jnp.where(early, 0, 1), jnp.where(k % 2 == 0, b, (k + 3) // 2)


def conv_terms(place_ref, feature_ref, taps_ref, part_ref, b):
    chans, wide = feature_ref.shape[1], taps_ref.shape[1]
    rows = chans // 8
    for c in range(2):
        half = slice(4 * c * rows, 4 * (c + 1) * rows)
        terms = dot_rows(feature_ref[:, half], taps_ref[...]).astype(BF)
        for y in range(4):
            group, slot = slot_of(place_ref, c, y, b)
            part_ref[group, slot, :, :wide] = terms[y * rows : (y + 1) * rows]


def proj_terms(place_ref, grad_ref, activ_ref, part_ref, b, sum_ref, order_ref):
    chans, wide = grad_ref.shape[1], activ_ref.shape[1]
    share = chans // 128
    sum_ref[:chans, :] = dot_rows(grad_ref[...], activ_ref[...])
    for c in range(2):
        for y in range(4):
            ordered = order_ref.at[c * 4 + y]
            for q in range(16):
                owner = owner_of(c, y, q)
                ordered[q * share : (q + 1) * share, :] = sum_ref[
                    owner * share : (owner + 1) * share, :
                ]
            group, slot = slot_of(place_ref, c, y, b)
            part_ref[group, slot, :, 3 * wide :] = ordered[...].astype(BF)


def backward(grad, saved, conv, proj, step, place):
    total, chans = grad.shape
    mids = conv.shape[-1]
    rows = 16 * (chans // 128)
    ins = [Plain(grad, anywhere=True)]
    for b in (1, 0):
        feature, slope_in, activ, slope = saved[b]
        ins += [Plain(proj, b), Plain(slope), Plain(feature), Plain(activ)]
        ins += [Flat(conv, b), Plain(slope_in)]

    def body(fetched, sent, place_ref, grown_ref, taps_ref, sum_ref, order_ref):
        (grad_ref,), queue = get_then(fetched[:1], []), fetched[1:]
        out, part = sent
        for b in (1, 0):
            mine, queue = queue[:6], queue[6:]
            out_ref = grown_ref if b == 1 else out.source
            proj_ref, slope_ref = get_then(mine[:2], mine[2:] if b == 1 else [])
            pull(grad_ref, proj_ref, slope_ref, taps_ref, step * 2**b)
            feature_ref, activ_ref = get_then(mine[2:4], [])
            conv_terms(place_ref, feature_ref, taps_ref, part.source, b)
            proj_terms(place_ref, grad_ref, activ_ref, part.source, b, sum_ref, order_ref)
            if b == 0:
                part.send()
            flat_ref, slope_in_ref = get_then(mine[4:], queue)
            grow(grad_ref, taps_ref, flat_ref, slope_in_ref, out_ref)
            grad_ref = out_ref
        out.send()

    return staged_call(
        body, "backward", ins, [((total, chans), None), ((4, 4, rows, 4 * mids), 4)],
        [
            pltpu.VMEM((total, chans), BF),
            pltpu.VMEM((total, 3 * mids), BF),
            pltpu.VMEM((chans + 8, mids), F32),
            pltpu.VMEM((9, rows, mids), F32),
        ],
        3, place,
    )


def to_rings(block):
    return lax.all_to_all(block, RING, 0, 0, tiled=True)


def passed(block, axis, distance):
    size = lax.axis_size(axis)
    return lax.ppermute(block, axis, [(i, (i + distance) % size) for i in range(size)])


def total_of(parts):
    out = parts[0].astype(F32)
    for part in parts[1:]:
        out = out + part.astype(F32)
    return out


def core_sum(mine, came, *at):
    return [total_of([mine[i], came[i]]).astype(BF) for i in at]


def column_sum(first, second, beside):
    two0, two1, right1, left0 = first
    own, right0, left1 = second
    two0, two1 = passed(two0, COLUMN, 1), passed(two1, COLUMN, -1)
    right1, left0 = passed(right1, COLUMN, 1), passed(left0, COLUMN, -1)
    right0 = passed(total_of([right0, two0]).astype(BF), COLUMN, 1)
    left1 = passed(total_of([left1, two1]).astype(BF), COLUMN, -1)
    right0, left1, beside = lax.optimization_barrier((right0, left1, beside))
    return total_of([own, jnp.stack([left0, right1]), jnp.stack([right0, left1])]).astype(BF), beside


def ring_step(rows, second):
    pieces = rows.reshape(2, 4, -1, rows.shape[-1])
    x, z, c = (lax.axis_index(axis) for axis in ("x", "z", "c"))
    me = jnp.where(c == second, x, z)

    def piece(k):
        return lax.dynamic_index_in_dim(pieces, (me + k) % 4, 1, keepdims=False)

    def sent(k):
        route = []
        for i in range(32):
            x, z, c = i // 8, i // 2 % 4, i % 2
            x, z = ((x + k) % 4, z) if c == second else (x, (z + k) % 4)
            route.append((i, (x * 4 + z) * 2 + c))
        return lax.ppermute(piece(k), ("x", "z", "c"), route)

    return total_of([piece(0)] + [sent(k) for k in (2, 1, 3)])


def local(inputs, cotangent, conv, proj):
    genomes, bins, chans = inputs.shape
    total = genomes * bins
    step = total // 16
    mids = conv.shape[-1]

    def rings(block):
        return to_rings(block.reshape(16, step, chans)).reshape(total, chans)

    def unring(block):
        return to_rings(block.reshape(16, step, chans)).reshape(genomes, bins, chans)

    place = [lax.axis_index("c"), lax.axis_index(COLUMN)]
    place = jnp.stack(place).astype(jnp.int32)
    state = rings(inputs)
    grad = rings(cotangent)
    out, saved = forward(state, conv, proj, step)
    outputs = unring(out)
    grad, *parts = backward(grad, saved, conv, proj, step, place)
    input_grad = unring(grad)
    came = [passed(part, "c", 1) for part in parts[2:]]
    *came, outputs = lax.optimization_barrier((*came, outputs))
    first = core_sum(parts[0], came[0], 0, 1)
    *first, rest = lax.optimization_barrier((*first, came[0]))
    first += core_sum(parts[0], rest, 2, 3)
    second = core_sum(parts[1], came[1], slice(2), 2, 3)
    share, input_grad = column_sum(first, second, input_grad)
    share = ring_step(share, 0).astype(BF)
    outputs, input_grad = settled(outputs), settled(input_grad)
    share, outputs, input_grad = lax.optimization_barrier((share, outputs, input_grad))
    share = ring_step(share, 1) * jnp.float32(1.0 / math.sqrt(total * 128))
    share = share.reshape(2, -1, 4, mids)
    conv_out = share[:, :, :3].transpose(0, 2, 1, 3)
    proj_out = share[:, :, 3].transpose(0, 2, 1)
    return outputs, input_grad, conv_out, proj_out


def solution(mesh):
    fine = Mesh(mesh.devices.reshape(4, 4, 2, 2, 2), ("x", "z", "yh", "c", "yl"))
    rows = P("yl", SEQ, None)
    in_specs = (rows, rows, P(), P())
    out_specs = (rows, rows, P(None, None, SEQ + ("yl",), None), P(None, None, SEQ + ("yl",)))
    return jax.shard_map(local, mesh=fine, in_specs=in_specs, out_specs=out_specs, check_vma=False)
```

```python
import functools
import math

import jax
import jax.numpy as jnp
import numpy as np
from jax import lax
from jax.experimental import pallas as pl
from jax.experimental.pallas import tpu as pltpu
from jax.sharding import Mesh
from jax.sharding import PartitionSpec as P

RING = ("x", "z")
COLUMN = ("yh", "yl")
SEQ = ("x", "z", "yh", "c")
BF = jnp.bfloat16
F32 = jnp.float32
BLOCK = 256
VMEM_BYTES = 52 * 1024 * 1024


def gelu_parts(value):
    cdf = 0.5 * (1.0 + lax.erf(value * (1.0 / math.sqrt(2.0))))
    density = jnp.exp(-0.5 * value * value) * (1.0 / math.sqrt(2.0 * math.pi))
    return (value * cdf).astype(BF), (cdf + value * density).astype(BF)


def dot(left, right):
    return jnp.dot(left, right, preferred_element_type=F32)


def dot_t(left, right):
    return lax.dot_general(left, right, (((1,), (1,)), ((), ())), preferred_element_type=F32)


def dot_rows(left, right):
    return lax.dot_general(left, right, (((0,), (0,)), ((), ())), preferred_element_type=F32)


def ring_rows(ref, start, count):
    total = ref.shape[0]
    start %= total
    if start + count <= total:
        return ref[start : start + count, :]
    first = total - start
    return jnp.concatenate([ref[start:total, :], ref[: count - first, :]], axis=0)


class Fetched:
    def __init__(self, copies, target):
        self.copies, self.target, self.here = copies, target, False

    def start(self):
        for copy in self.copies:
            copy.start()

    def get(self):
        if not self.here:
            for copy in self.copies:
                copy.wait()
            self.here = True
        return self.target


class Sent:
    def __init__(self, source, copies):
        self.source, self.copies = source, copies

    def send(self):
        for copy in self.copies:
            copy.start()

    def finish(self):
        for copy in self.copies:
            copy.wait()


def get_then(wanted, following):
    refs = [f.get() for f in wanted]
    for f in following:
        f.start()
    return refs


class Flat:
    def __init__(self, array, b):
        self.array, self.b = array, b
        taps, chans, mids = array.shape[1:]
        self.shape = (chans, taps * mids)

    def copies(self, source, target, sems):
        mids = self.array.shape[-1]
        return [
            pltpu.make_async_copy(
                source.at[self.b, k], target.at[:, k * mids : (k + 1) * mids], sems.at[k]
            )
            for k in range(3)
        ]


class Plain:
    def __init__(self, array, b=None, anywhere=False):
        self.array, self.b, self.anywhere = array, b, anywhere
        self.shape = array.shape if b is None else array.shape[1:]

    def copies(self, source, target, sems):
        source = source if self.b is None else source.at[self.b]
        return [pltpu.make_async_copy(source, target, sems.at[0])]


def staged_call(body, name, ins, outs, scratch, urgent, place=None):
    kept_outs = [pltpu.VMEM(shape, BF) for shape, _ in outs]
    held = [pltpu.VMEM(x.shape, BF) for x in ins] + kept_outs
    results = [(i, k) for i, (_, count) in enumerate(outs) for k in range(count or 1)]
    n, m, held_n = len(ins), len(results), len(held)
    extra = [] if place is None else [place]

    def kernel(*refs):
        head, refs = refs[: len(extra)], refs[len(extra) :]
        sources, targets, kept = refs[:n], refs[n : n + m], refs[n + m : n + m + held_n]
        in_sems, out_sems = refs[n + m + held_n], refs[n + m + held_n + 1]
        rest = refs[n + m + held_n + 2 :]
        fetched = [
            Fetched(x.copies(sources[i], kept[i], in_sems.at[i]), kept[i])
            for i, x in enumerate(ins)
        ]
        for f in fetched[:urgent]:
            f.start()
        sent = [Sent(kept[n + i], []) for i in range(len(outs))]
        for j, (i, k) in enumerate(results):
            source = kept[n + i] if outs[i][1] is None else kept[n + i].at[k]
            sent[i].copies.append(pltpu.make_async_copy(source, targets[j], out_sems.at[j]))
        body(fetched, sent, *head, *rest)
        for result in sent:
            result.finish()

    def out_shape(i):
        shape, count = outs[i]
        return pltpu.HBM(shape if count is None else shape[1:], BF)

    return pl.pallas_call(
        kernel,
        out_shape=[out_shape(i) for i, _ in results],
        in_specs=[pl.BlockSpec(memory_space=pltpu.SMEM)] * len(extra)
        + [pl.BlockSpec(memory_space=pl.ANY if anywhere(x) else pltpu.HBM) for x in ins],
        out_specs=[pl.BlockSpec(memory_space=pltpu.HBM)] * m,
        scratch_shapes=held
        + [pltpu.SemaphoreType.DMA((n, 3)), pltpu.SemaphoreType.DMA((m,))]
        + list(scratch),
        compiler_params=pltpu.CompilerParams(vmem_limit_bytes=VMEM_BYTES),
        cost_estimate=pl.CostEstimate(flops=1, bytes_accessed=1, transcendentals=0),
        name=name,
    )(
        *extra,
        *[
            x.array if anywhere(x) else pltpu.with_memory_space_constraint(x.array, pltpu.HBM)
            for x in ins
        ],
    )


def anywhere(operand):
    return getattr(operand, "anywhere", False)


def settled(array):
    return array * lax.optimization_barrier(jnp.ones((), array.dtype))


def owner_of(c, y, q):
    ring = q if c == 0 else q % 4 * 4 + q // 4
    return ((ring * 2 + y // 2) * 2 + c) * 2 + y % 2


def order_of(chans):
    share = chans // 128
    owners = [owner_of(c, y, q) for c in range(2) for y in range(4) for q in range(16)]
    source = np.repeat(np.array(owners) * share, share) + np.tile(np.arange(share), 128)
    return jnp.asarray(np.arange(chans)[:, None] == source[None, :], BF)


def forward(state, conv, proj, step):
    total, chans = state.shape
    mids = conv.shape[-1]
    wide, thin = ((total, chans), None), ((total, mids), None)
    starts = range(0, total, BLOCK)

    def body(fetched, sent, mid_ref, *feature_refs):
        out, saved = sent[0], (sent[1:5], sent[5:9])

        def enter(b, start, value):
            rows = slice(start, start + BLOCK)
            feature, slope = gelu_parts(value)
            feature_refs[b][rows, :] = feature
            saved[b][0].source[rows, :] = dot(feature, order_ref[...]).astype(BF)
            saved[b][1].source[rows, :] = slope

        x_ref, order_ref = get_then(fetched[:2], fetched[2:])
        for start in starts:
            enter(0, start, x_ref[start : start + BLOCK, :].astype(F32))
        saved[0][0].send()
        saved[0][1].send()
        for b in range(2):
            feature_ref = feature_refs[b]
            activ_ref, slope_ref = saved[b][2].source, saved[b][3].source
            conv_ref, proj_ref = (f.get() for f in fetched[2 + 2 * b : 4 + 2 * b])
            source = x_ref if b == 0 else mid_ref
            shift = step * 2**b
            for start in starts:
                rows = slice(start, start + BLOCK)
                pre = (
                    dot(ring_rows(feature_ref, start - shift, BLOCK), conv_ref[0])
                    + dot(feature_ref[rows, :], conv_ref[1])
                    + dot(ring_rows(feature_ref, start + shift, BLOCK), conv_ref[2])
                )
                activ, slope = gelu_parts(pre)
                activ_ref[rows, :] = activ
                slope_ref[rows, :] = slope
                after = source[rows, :].astype(F32) + dot(activ, proj_ref[...])
                after = after.astype(BF)
                if b == 0:
                    mid_ref[rows, :] = after
                    enter(1, start, after.astype(F32))
                else:
                    out.source[rows, :] = after
            for result in saved[0][2:] + saved[1][:2] if b == 0 else [*saved[1][2:], out]:
                result.send()

    outs = staged_call(
        body, "forward",
        [Plain(state, anywhere=True), Plain(order_of(chans))]
        + [Plain(x, b) for b in range(2) for x in (conv, proj)],
        [wide] + [wide, wide, thin, thin] * 2, [pltpu.VMEM((total, chans), BF)] * 3, 2,
    )
    return outs[0], (outs[1:5], outs[5:9])


def put_ring_rows(ref, start, columns, value):
    total, count = ref.shape[0], value.shape[0]
    start %= total
    first = min(count, total - start)
    ref[start : start + first, columns] = value[:first]
    if first < count:
        ref[: count - first, columns] = value[first:]


def pull(from_ref, proj_ref, slope_ref, taps_ref, shift):
    total, mids = slope_ref.shape
    for start in range(0, total, BLOCK):
        rows = slice(start, start + BLOCK)
        pulled = dot_t(from_ref[rows, :], proj_ref[...])
        e = (pulled * slope_ref[rows, :].astype(F32)).astype(BF)
        for k in range(3):
            columns = slice(k * mids, (k + 1) * mids)
            put_ring_rows(taps_ref, start + (k - 1) * shift, columns, e)


def grow(from_ref, taps_ref, flat_ref, slope_ref, out_ref):
    for start in range(0, from_ref.shape[0], BLOCK):
        rows = slice(start, start + BLOCK)
        summed = dot_t(taps_ref[rows, :], flat_ref[...])
        grown = from_ref[rows, :].astype(F32) + summed * slope_ref[rows, :].astype(F32)
        out_ref[rows, :] = grown.astype(BF)


def slot_of(place_ref, c, y, b):
    half, k = (c + place_ref[0]) % 2, (y + 4 - place_ref[1]) % 4
    early = (k >= 2) if b == 0 else (k == 1) | (k == 2)
    return half * 2 + jnp.where(early, 0, 1), jnp.where(k % 2 == 0, b, (k + 3) // 2)


def conv_terms(place_ref, feature_ref, taps_ref, part_ref, b):
    chans, wide = feature_ref.shape[1], taps_ref.shape[1]
    rows = chans // 8
    for c in range(2):
        half = slice(4 * c * rows, 4 * (c + 1) * rows)
        terms = dot_rows(feature_ref[:, half], taps_ref[...]).astype(BF)
        for y in range(4):
            group, slot = slot_of(place_ref, c, y, b)
            part_ref[group, slot, :, :wide] = terms[y * rows : (y + 1) * rows]


def proj_terms(place_ref, grad_ref, activ_ref, part_ref, b, sum_ref, order_ref):
    chans, wide = grad_ref.shape[1], activ_ref.shape[1]
    share = chans // 128
    sum_ref[:chans, :] = dot_rows(grad_ref[...], activ_ref[...])
    for c in range(2):
        for y in range(4):
            ordered = order_ref.at[c * 4 + y]
            for q in range(16):
                owner = owner_of(c, y, q)
                ordered[q * share : (q + 1) * share, :] = sum_ref[
                    owner * share : (owner + 1) * share, :
                ]
            group, slot = slot_of(place_ref, c, y, b)
            part_ref[group, slot, :, 3 * wide :] = ordered[...].astype(BF)


def backward(grad, saved, conv, proj, step, place):
    total, chans = grad.shape
    mids = conv.shape[-1]
    rows = 16 * (chans // 128)
    ins = [Plain(grad, anywhere=True)]
    for b in (1, 0):
        feature, slope_in, activ, slope = saved[b]
        ins += [Plain(proj, b), Plain(slope), Plain(feature), Plain(activ)]
        ins += [Flat(conv, b), Plain(slope_in)]

    def body(fetched, sent, place_ref, grown_ref, taps_ref, sum_ref, order_ref):
        (grad_ref,), queue = get_then(fetched[:1], []), fetched[1:]
        out, part = sent
        for b in (1, 0):
            mine, queue = queue[:6], queue[6:]
            out_ref = grown_ref if b == 1 else out.source
            proj_ref, slope_ref = get_then(mine[:2], mine[2:] if b == 1 else [])
            pull(grad_ref, proj_ref, slope_ref, taps_ref, step * 2**b)
            feature_ref, activ_ref = get_then(mine[2:4], [])
            conv_terms(place_ref, feature_ref, taps_ref, part.source, b)
            proj_terms(place_ref, grad_ref, activ_ref, part.source, b, sum_ref, order_ref)
            if b == 0:
                part.send()
            flat_ref, slope_in_ref = get_then(mine[4:], queue)
            grow(grad_ref, taps_ref, flat_ref, slope_in_ref, out_ref)
            grad_ref = out_ref
        out.send()

    return staged_call(
        body, "backward", ins, [((total, chans), None), ((4, 4, rows, 4 * mids), 4)],
        [
            pltpu.VMEM((total, chans), BF),
            pltpu.VMEM((total, 3 * mids), BF),
            pltpu.VMEM((chans + 8, mids), F32),
            pltpu.VMEM((9, rows, mids), F32),
        ],
        3, place,
    )


def to_rings(block):
    return lax.all_to_all(block, RING, 0, 0, tiled=True)


def passed(block, axis, distance):
    size = lax.axis_size(axis)
    return lax.ppermute(block, axis, [(i, (i + distance) % size) for i in range(size)])


def total_of(parts):
    out = parts[0].astype(F32)
    for part in parts[1:]:
        out = out + part.astype(F32)
    return out


def core_sum(mine, came, *at):
    return [total_of([mine[i], came[i]]).astype(BF) for i in at]


def column_sum(first, second, beside):
    two0, two1, right1, left0 = first
    own, right0, left1 = second
    two0, two1 = passed(two0, COLUMN, 1), passed(two1, COLUMN, -1)
    right1, left0 = passed(right1, COLUMN, 1), passed(left0, COLUMN, -1)
    right0 = passed(total_of([right0, two0]).astype(BF), COLUMN, 1)
    left1 = passed(total_of([left1, two1]).astype(BF), COLUMN, -1)
    right0, left1, beside = lax.optimization_barrier((right0, left1, beside))
    return total_of([own, jnp.stack([left0, right1]), jnp.stack([right0, left1])]).astype(BF), beside


def ring_step(rows, second):
    pieces = rows.reshape(2, 4, -1, rows.shape[-1])
    x, z, c = (lax.axis_index(axis) for axis in ("x", "z", "c"))
    me = jnp.where(c == second, x, z)

    def piece(k):
        return lax.dynamic_index_in_dim(pieces, (me + k) % 4, 1, keepdims=False)

    def sent(k):
        route = []
        for i in range(32):
            x, z, c = i // 8, i // 2 % 4, i % 2
            x, z = ((x + k) % 4, z) if c == second else (x, (z + k) % 4)
            route.append((i, (x * 4 + z) * 2 + c))
        return lax.ppermute(piece(k), ("x", "z", "c"), route)

    return total_of([piece(0)] + [sent(k) for k in (1, 3, 2)])


def local(inputs, cotangent, conv, proj):
    genomes, bins, chans = inputs.shape
    total = genomes * bins
    step = total // 16
    mids = conv.shape[-1]

    def rings(block):
        return to_rings(block.reshape(16, step, chans)).reshape(total, chans)

    def unring(block):
        return to_rings(block.reshape(16, step, chans)).reshape(genomes, bins, chans)

    place = [lax.axis_index("c"), lax.axis_index(COLUMN)]
    place = jnp.stack(place).astype(jnp.int32)
    state = rings(inputs)
    grad = rings(cotangent)
    out, saved = forward(state, conv, proj, step)
    outputs = unring(out)
    grad, *parts = backward(grad, saved, conv, proj, step, place)
    input_grad = unring(grad)
    came = [passed(part, "c", 1) for part in parts[2:]]
    *came, outputs = lax.optimization_barrier((*came, outputs))
    first = core_sum(parts[0], came[0], 0, 1)
    *first, rest = lax.optimization_barrier((*first, came[0]))
    first += core_sum(parts[0], rest, 2, 3)
    second = core_sum(parts[1], came[1], slice(2), 2, 3)
    share, input_grad = column_sum(first, second, input_grad)
    share = ring_step(share, 0).astype(BF)
    outputs, input_grad = settled(outputs), settled(input_grad)
    share, outputs, input_grad = lax.optimization_barrier((share, outputs, input_grad))
    share = ring_step(share, 1) * jnp.float32(1.0 / math.sqrt(total * 128))
    share = share.reshape(2, -1, 4, mids)
    conv_out = share[:, :, :3].transpose(0, 2, 1, 3)
    proj_out = share[:, :, 3].transpose(0, 2, 1)
    return outputs, input_grad, conv_out, proj_out


def solution(mesh):
    fine = Mesh(mesh.devices.reshape(4, 4, 2, 2, 2), ("x", "z", "yh", "c", "yl"))
    rows = P("yl", SEQ, None)
    in_specs = (rows, rows, P(), P())
    out_specs = (rows, rows, P(None, None, SEQ + ("yl",), None), P(None, None, SEQ + ("yl",)))
    return jax.shard_map(local, mesh=fine, in_specs=in_specs, out_specs=out_specs, check_vma=False)
```

```python
import functools
import math

import jax
import jax.numpy as jnp
import numpy as np
from jax import lax
from jax.experimental import pallas as pl
from jax.experimental.pallas import tpu as pltpu
from jax.sharding import Mesh
from jax.sharding import PartitionSpec as P

RING = ("x", "z")
COLUMN = ("yh", "yl")
SEQ = ("x", "z", "yh", "c")
BF = jnp.bfloat16
F32 = jnp.float32
BLOCK = 256
VMEM_BYTES = 52 * 1024 * 1024


def gelu_parts(value):
    cdf = 0.5 * (1.0 + lax.erf(value * (1.0 / math.sqrt(2.0))))
    density = jnp.exp(-0.5 * value * value) * (1.0 / math.sqrt(2.0 * math.pi))
    return (value * cdf).astype(BF), (cdf + value * density).astype(BF)


def dot(left, right):
    return jnp.dot(left, right, preferred_element_type=F32)


def dot_t(left, right):
    return lax.dot_general(left, right, (((1,), (1,)), ((), ())), preferred_element_type=F32)


def dot_rows(left, right):
    return lax.dot_general(left, right, (((0,), (0,)), ((), ())), preferred_element_type=F32)


def ring_rows(ref, start, count):
    total = ref.shape[0]
    start %= total
    if start + count <= total:
        return ref[start : start + count, :]
    first = total - start
    return jnp.concatenate([ref[start:total, :], ref[: count - first, :]], axis=0)


class Fetched:
    def __init__(self, copies, target):
        self.copies, self.target, self.here = copies, target, False

    def start(self):
        for copy in self.copies:
            copy.start()

    def get(self):
        if not self.here:
            for copy in self.copies:
                copy.wait()
            self.here = True
        return self.target


class Sent:
    def __init__(self, source, copies):
        self.source, self.copies = source, copies

    def send(self):
        for copy in self.copies:
            copy.start()

    def finish(self):
        for copy in self.copies:
            copy.wait()


def get_then(wanted, following):
    refs = [f.get() for f in wanted]
    for f in following:
        f.start()
    return refs


class Flat:
    def __init__(self, array, b):
        self.array, self.b = array, b
        taps, chans, mids = array.shape[1:]
        self.shape = (chans, taps * mids)

    def copies(self, source, target, sems):
        mids = self.array.shape[-1]
        return [
            pltpu.make_async_copy(
                source.at[self.b, k], target.at[:, k * mids : (k + 1) * mids], sems.at[k]
            )
            for k in range(3)
        ]


class Plain:
    def __init__(self, array, b=None, anywhere=False):
        self.array, self.b, self.anywhere = array, b, anywhere
        self.shape = array.shape if b is None else array.shape[1:]

    def copies(self, source, target, sems):
        source = source if self.b is None else source.at[self.b]
        return [pltpu.make_async_copy(source, target, sems.at[0])]


def staged_call(body, name, ins, outs, scratch, urgent, place=None):
    kept_outs = [pltpu.VMEM(shape, BF) for shape, _ in outs]
    held = [pltpu.VMEM(x.shape, BF) for x in ins] + kept_outs
    results = [(i, k) for i, (_, count) in enumerate(outs) for k in range(count or 1)]
    n, m, held_n = len(ins), len(results), len(held)
    extra = [] if place is None else [place]

    def kernel(*refs):
        head, refs = refs[: len(extra)], refs[len(extra) :]
        sources, targets, kept = refs[:n], refs[n : n + m], refs[n + m : n + m + held_n]
        in_sems, out_sems = refs[n + m + held_n], refs[n + m + held_n + 1]
        rest = refs[n + m + held_n + 2 :]
        fetched = [
            Fetched(x.copies(sources[i], kept[i], in_sems.at[i]), kept[i])
            for i, x in enumerate(ins)
        ]
        for f in fetched[:urgent]:
            f.start()
        sent = [Sent(kept[n + i], []) for i in range(len(outs))]
        for j, (i, k) in enumerate(results):
            source = kept[n + i] if outs[i][1] is None else kept[n + i].at[k]
            sent[i].copies.append(pltpu.make_async_copy(source, targets[j], out_sems.at[j]))
        body(fetched, sent, *head, *rest)
        for result in sent:
            result.finish()

    def out_shape(i):
        shape, count = outs[i]
        return pltpu.HBM(shape if count is None else shape[1:], BF)

    return pl.pallas_call(
        kernel,
        out_shape=[out_shape(i) for i, _ in results],
        in_specs=[pl.BlockSpec(memory_space=pltpu.SMEM)] * len(extra)
        + [pl.BlockSpec(memory_space=pl.ANY if anywhere(x) else pltpu.HBM) for x in ins],
        out_specs=[pl.BlockSpec(memory_space=pltpu.HBM)] * m,
        scratch_shapes=held
        + [pltpu.SemaphoreType.DMA((n, 3)), pltpu.SemaphoreType.DMA((m,))]
        + list(scratch),
        compiler_params=pltpu.CompilerParams(vmem_limit_bytes=VMEM_BYTES),
        cost_estimate=pl.CostEstimate(flops=1, bytes_accessed=1, transcendentals=0),
        name=name,
    )(
        *extra,
        *[
            x.array if anywhere(x) else pltpu.with_memory_space_constraint(x.array, pltpu.HBM)
            for x in ins
        ],
    )


def anywhere(operand):
    return getattr(operand, "anywhere", False)


def settled(array):
    return array * lax.optimization_barrier(jnp.ones((), array.dtype))


def owner_of(c, y, q):
    ring = q if c == 0 else q % 4 * 4 + q // 4
    return ((ring * 2 + y // 2) * 2 + c) * 2 + y % 2


def order_of(chans):
    share = chans // 128
    owners = [owner_of(c, y, q) for c in range(2) for y in range(4) for q in range(16)]
    source = np.repeat(np.array(owners) * share, share) + np.tile(np.arange(share), 128)
    return jnp.asarray(np.arange(chans)[:, None] == source[None, :], BF)


def forward(state, conv, proj, step):
    total, chans = state.shape
    mids = conv.shape[-1]
    wide, thin = ((total, chans), None), ((total, mids), None)
    starts = range(0, total, BLOCK)

    def body(fetched, sent, mid_ref, *feature_refs):
        out, saved = sent[0], (sent[1:5], sent[5:9])

        def enter(b, start, value):
            rows = slice(start, start + BLOCK)
            feature, slope = gelu_parts(value)
            feature_refs[b][rows, :] = feature
            saved[b][0].source[rows, :] = dot(feature, order_ref[...]).astype(BF)
            saved[b][1].source[rows, :] = slope

        x_ref, order_ref = get_then(fetched[:2], fetched[2:])
        for start in starts:
            enter(0, start, x_ref[start : start + BLOCK, :].astype(F32))
        saved[0][0].send()
        saved[0][1].send()
        for b in range(2):
            feature_ref = feature_refs[b]
            activ_ref, slope_ref = saved[b][2].source, saved[b][3].source
            conv_ref, proj_ref = (f.get() for f in fetched[2 + 2 * b : 4 + 2 * b])
            source = x_ref if b == 0 else mid_ref
            shift = step * 2**b
            for start in starts:
                rows = slice(start, start + BLOCK)
                pre = (
                    dot(ring_rows(feature_ref, start - shift, BLOCK), conv_ref[0])
                    + dot(feature_ref[rows, :], conv_ref[1])
                    + dot(ring_rows(feature_ref, start + shift, BLOCK), conv_ref[2])
                )
                activ, slope = gelu_parts(pre)
                activ_ref[rows, :] = activ
                slope_ref[rows, :] = slope
                after = source[rows, :].astype(F32) + dot(activ, proj_ref[...])
                after = after.astype(BF)
                if b == 0:
                    mid_ref[rows, :] = after
                    enter(1, start, after.astype(F32))
                else:
                    out.source[rows, :] = after
            for result in saved[0][2:] + saved[1][:2] if b == 0 else [*saved[1][2:], out]:
                result.send()

    outs = staged_call(
        body, "forward",
        [Plain(state, anywhere=True), Plain(order_of(chans))]
        + [Plain(x, b) for b in range(2) for x in (conv, proj)],
        [wide] + [wide, wide, thin, thin] * 2, [pltpu.VMEM((total, chans), BF)] * 3, 2,
    )
    return outs[0], (outs[1:5], outs[5:9])


def put_ring_rows(ref, start, columns, value):
    total, count = ref.shape[0], value.shape[0]
    start %= total
    first = min(count, total - start)
    ref[start : start + first, columns] = value[:first]
    if first < count:
        ref[: count - first, columns] = value[first:]


def pull(from_ref, proj_ref, slope_ref, taps_ref, shift):
    total, mids = slope_ref.shape
    for start in range(0, total, BLOCK):
        rows = slice(start, start + BLOCK)
        pulled = dot_t(from_ref[rows, :], proj_ref[...])
        e = (pulled * slope_ref[rows, :].astype(F32)).astype(BF)
        for k in range(3):
            columns = slice(k * mids, (k + 1) * mids)
            put_ring_rows(taps_ref, start + (k - 1) * shift, columns, e)


def grow(from_ref, taps_ref, flat_ref, slope_ref, out_ref):
    for start in range(0, from_ref.shape[0], BLOCK):
        rows = slice(start, start + BLOCK)
        summed = dot_t(taps_ref[rows, :], flat_ref[...])
        grown = from_ref[rows, :].astype(F32) + summed * slope_ref[rows, :].astype(F32)
        out_ref[rows, :] = grown.astype(BF)


def slot_of(place_ref, c, y, b):
    half, k = (c + place_ref[0]) % 2, (y + 4 - place_ref[1]) % 4
    early = (k >= 2) if b == 0 else (k == 1) | (k == 2)
    return half * 2 + jnp.where(early, 0, 1), jnp.where(k % 2 == 0, b, (k + 3) // 2)


def conv_terms(place_ref, feature_ref, taps_ref, part_ref, b):
    chans, wide = feature_ref.shape[1], taps_ref.shape[1]
    rows = chans // 8
    for c in range(2):
        half = slice(4 * c * rows, 4 * (c + 1) * rows)
        terms = dot_rows(feature_ref[:, half], taps_ref[...]).astype(BF)
        for y in range(4):
            group, slot = slot_of(place_ref, c, y, b)
            part_ref[group, slot, :, :wide] = terms[y * rows : (y + 1) * rows]


def proj_terms(place_ref, grad_ref, activ_ref, part_ref, b, sum_ref, order_ref):
    chans, wide = grad_ref.shape[1], activ_ref.shape[1]
    share = chans // 128
    sum_ref[:chans, :] = dot_rows(grad_ref[...], activ_ref[...])
    for c in range(2):
        for y in range(4):
            ordered = order_ref.at[c * 4 + y]
            for q in range(16):
                owner = owner_of(c, y, q)
                ordered[q * share : (q + 1) * share, :] = sum_ref[
                    owner * share : (owner + 1) * share, :
                ]
            group, slot = slot_of(place_ref, c, y, b)
            part_ref[group, slot, :, 3 * wide :] = ordered[...].astype(BF)


def backward(grad, saved, conv, proj, step, place):
    total, chans = grad.shape
    mids = conv.shape[-1]
    rows = 16 * (chans // 128)
    ins = [Plain(grad, anywhere=True)]
    for b in (1, 0):
        feature, slope_in, activ, slope = saved[b]
        ins += [Plain(proj, b), Plain(slope), Plain(feature), Plain(activ)]
        ins += [Flat(conv, b), Plain(slope_in)]

    def body(fetched, sent, place_ref, grown_ref, taps_ref, sum_ref, order_ref):
        (grad_ref,), queue = get_then(fetched[:1], []), fetched[1:]
        out, part = sent
        for b in (1, 0):
            mine, queue = queue[:6], queue[6:]
            out_ref = grown_ref if b == 1 else out.source
            proj_ref, slope_ref = get_then(mine[:2], mine[2:] if b == 1 else [])
            pull(grad_ref, proj_ref, slope_ref, taps_ref, step * 2**b)
            feature_ref, activ_ref = get_then(mine[2:4], [])
            conv_terms(place_ref, feature_ref, taps_ref, part.source, b)
            proj_terms(place_ref, grad_ref, activ_ref, part.source, b, sum_ref, order_ref)
            if b == 0:
                part.send()
            flat_ref, slope_in_ref = get_then(mine[4:], queue)
            grow(grad_ref, taps_ref, flat_ref, slope_in_ref, out_ref)
            grad_ref = out_ref
        out.send()

    return staged_call(
        body, "backward", ins, [((total, chans), None), ((4, 4, rows, 4 * mids), 4)],
        [
            pltpu.VMEM((total, chans), BF),
            pltpu.VMEM((total, 3 * mids), BF),
            pltpu.VMEM((chans + 8, mids), F32),
            pltpu.VMEM((9, rows, mids), F32),
        ],
        3, place,
    )


def to_rings(block):
    return lax.all_to_all(block, RING, 0, 0, tiled=True)


def passed(block, axis, distance):
    size = lax.axis_size(axis)
    return lax.ppermute(block, axis, [(i, (i + distance) % size) for i in range(size)])


def total_of(parts):
    out = parts[0].astype(F32)
    for part in parts[1:]:
        out = out + part.astype(F32)
    return out


def core_sum(mine, came, *at):
    return [total_of([mine[i], came[i]]).astype(BF) for i in at]


def column_sum(first, second, beside):
    two0, two1, right1, left0 = first
    own, right0, left1 = second
    two0, two1 = passed(two0, COLUMN, 1), passed(two1, COLUMN, -1)
    right1, left0 = passed(right1, COLUMN, 1), passed(left0, COLUMN, -1)
    right0 = passed(total_of([right0, two0]).astype(BF), COLUMN, 1)
    left1 = passed(total_of([left1, two1]).astype(BF), COLUMN, -1)
    near = lax.optimization_barrier(total_of([own, jnp.stack([left0, right1])]).astype(BF))
    right0, left1, beside = lax.optimization_barrier((right0, left1, beside))
    return total_of([near, jnp.stack([right0, left1])]).astype(BF), beside


def ring_step(rows, second):
    pieces = rows.reshape(2, 4, -1, rows.shape[-1])
    x, z, c = (lax.axis_index(axis) for axis in ("x", "z", "c"))
    me = jnp.where(c == second, x, z)

    def piece(k):
        return lax.dynamic_index_in_dim(pieces, (me + k) % 4, 1, keepdims=False)

    def sent(k):
        route = []
        for i in range(32):
            x, z, c = i // 8, i // 2 % 4, i % 2
            x, z = ((x + k) % 4, z) if c == second else (x, (z + k) % 4)
            route.append((i, (x * 4 + z) * 2 + c))
        return lax.ppermute(piece(k), ("x", "z", "c"), route)

    return total_of([piece(0)] + [sent(k) for k in (1, 3, 2)])


def local(inputs, cotangent, conv, proj):
    genomes, bins, chans = inputs.shape
    total = genomes * bins
    step = total // 16
    mids = conv.shape[-1]

    def rings(block):
        return to_rings(block.reshape(16, step, chans)).reshape(total, chans)

    def unring(block):
        return to_rings(block.reshape(16, step, chans)).reshape(genomes, bins, chans)

    place = [lax.axis_index("c"), lax.axis_index(COLUMN)]
    place = jnp.stack(place).astype(jnp.int32)
    state = rings(inputs)
    grad = rings(cotangent)
    out, saved = forward(state, conv, proj, step)
    outputs = unring(out)
    grad, *parts = backward(grad, saved, conv, proj, step, place)
    input_grad = unring(grad)
    came = [passed(part, "c", 1) for part in parts[2:]]
    *came, outputs = lax.optimization_barrier((*came, outputs))
    first = core_sum(parts[0], came[0], 0, 1)
    *first, rest = lax.optimization_barrier((*first, came[0]))
    first += core_sum(parts[0], rest, 2, 3)
    second = core_sum(parts[1], came[1], slice(2), 2, 3)
    share, input_grad = column_sum(first, second, input_grad)
    share = ring_step(share, 0).astype(BF)
    outputs, input_grad = settled(outputs), settled(input_grad)
    share, outputs, input_grad = lax.optimization_barrier((share, outputs, input_grad))
    share = ring_step(share, 1) * jnp.float32(1.0 / math.sqrt(total * 128))
    share = share.reshape(2, -1, 4, mids)
    conv_out = share[:, :, :3].transpose(0, 2, 1, 3)
    proj_out = share[:, :, 3].transpose(0, 2, 1)
    return outputs, input_grad, conv_out, proj_out


def solution(mesh):
    fine = Mesh(mesh.devices.reshape(4, 4, 2, 2, 2), ("x", "z", "yh", "c", "yl"))
    rows = P("yl", SEQ, None)
    in_specs = (rows, rows, P(), P())
    out_specs = (rows, rows, P(None, None, SEQ + ("yl",), None), P(None, None, SEQ + ("yl",)))
    return jax.shard_map(local, mesh=fine, in_specs=in_specs, out_specs=out_specs, check_vma=False)
```
